256 devices in a mesh: grp: 8 (over z), dev: 32 (over x, y, core).
Axes of the slice: x: 4, y: 4, z: 8, core: 2. Of those that a mesh axis runs over, the one named last changes fastest.
Arguments:
- node_rows: bfloat16 [196608, 1024], P(('grp', 'dev')), may hold values from -6 to 6
- w_self: bfloat16 [1024, 1024], replicated, may hold values from -0.1875 to 0.1875
- w_neigh: bfloat16 [1024, 1024], replicated, may hold values from -0.1875 to 0.1875
- hub_ids: int32 [64], replicated, may hold values from 0 to 196607, as said below
- bnd_idx: int32 [256, 32], P(('grp', 'dev')), may hold values from 0 to 767, as said below
- send_pos: int32 [256, 32, 64], P(('grp', 'dev')), may hold values from 0 to 31
- edge_src: int32 [1572864], P(('grp', 'dev')), may hold values from 0 to 2879, as said below
- edge_dst: int32 [1572864], P(('grp', 'dev')), may hold values from 0 to 767, as said below
Outputs:
- updated: bfloat16 [196608, 1024], P(('grp', 'dev'))
The draws below stay inside these ranges and needn't reach their ends.
Inputs may be any that keep to these rules, and one draw needn't show every extreme that they name: `hub_ids`: distinct global node ids; no device owns more than 2 hubs, and some own exactly 2. `bnd_idx`: the 32 entries of each device are distinct local rows. `edge_src`: an entry below 768 is a local row; 768 + j * 64 + s is halo slot s from peer j; 2816 + k is hub k. `edge_dst`: every local node is the destination of at least one edge of its device.
All inputs are finite; a program needn't handle non-finite values.
Results may differ from the reference program's by a relative error of at most 0.0026.
Values may be sent and summed in bfloat16 or wider, within the bound.
A program may use at most 128 MiB of HBM per device.

```python
import jax
import jax.numpy as jnp
from jax import lax

D = 1024
NPD = 768
HUBS = 64
HUB_MOST = 2
BND = 32
SLOT = 64
E_DEV = 6144
NODES = 196608
EDGES = 1572864
N_DEV = 32
DEVICES = 256


def draw_hub_ids(key, part):
    key = jax.random.fold_in(key, 11)
    key_owner, key_row, key_order = jax.random.split(key, 3)
    owner_count = HUBS // HUB_MOST
    owners = jax.random.permutation(key_owner, NODES // NPD)[:owner_count]
    span = NPD // HUB_MOST
    offsets = jax.random.randint(key_row, (owner_count, HUB_MOST), 0, span)
    local_rows = offsets + jnp.arange(HUB_MOST, dtype=jnp.int32)[None, :] * span
    global_ids = (owners[:, None] * NPD + local_rows).reshape(-1)
    return jax.random.permutation(key_order, global_ids).astype(jnp.int32)


def draw_bnd_idx(key, part):
    key = jax.random.fold_in(key, 23)
    keys = jax.random.split(key, NODES // NPD)

    def choose(device_key):
        return jax.random.permutation(device_key, NPD)[:BND]
    return jax.vmap(choose)(keys).astype(jnp.int32)


def draw_edge_src(key, part):
    key = jax.random.fold_in(key, 37)
    key_kind, key_local, key_halo, key_hub = jax.random.split(key, 4)
    kinds = jax.random.randint(key_kind, (EDGES,), 0, 8)
    local_src = jax.random.randint(key_local, (EDGES,), 0, NPD)
    halo_src = NPD + jax.random.randint(key_halo, (EDGES,), 0, N_DEV * SLOT)
    hub_src = NPD + N_DEV * SLOT + jax.random.randint(key_hub, (EDGES,), 0, HUBS)
    chosen = jnp.where(kinds < 4, local_src, jnp.where(kinds < 6, halo_src, hub_src))
    return chosen.astype(jnp.int32)


def draw_edge_dst(key, part):
    key = jax.random.fold_in(key, 41)
    keys = jax.random.split(key, NODES // NPD)

    def targets(device_key):
        key_cover, key_rest = jax.random.split(device_key)
        cover = jax.random.permutation(key_cover, NPD)
        rest = jax.random.randint(key_rest, (E_DEV - NPD,), 0, NPD)
        return jnp.concatenate([cover, rest])
    return jax.vmap(targets)(keys).reshape(-1).astype(jnp.int32)


def plant(entries, own_key, smallest, high):
    shape = entries.shape
    spot = [jax.random.randint(jax.random.fold_in(own_key, axis), (), 0, shape[axis]) for axis in range(len(shape))]
    entries = entries.at[tuple(spot)].set(smallest)
    longest = shape.index(max(shape))
    spot[longest] = (spot[longest] + 1) % shape[longest]
    return entries.at[tuple(spot)].set(high)


def shard_levels(rng, shape, pieces, low, high):
    factor_of, own = 1.0, jax.random.fold_in(rng, 6)
    for axis_at, shards_of in pieces:
        steps = jnp.exp(jax.random.uniform(jax.random.fold_in(own, axis_at), (shards_of,), jnp.float32, low / len(pieces), high / len(pieces)))
        factor_of = factor_of * jnp.repeat(steps, shape[axis_at] // shards_of).reshape([-1 if axis == axis_at else 1 for axis in range(len(shape))])
    return factor_of


def bell_draw(own_key, shape, scale, limit, pieces=(), held_as=jnp.bfloat16):
    entries = jax.random.normal(own_key, shape, jnp.float32) * scale
    if len(pieces) > 0:
        entries = shard_levels(own_key, shape, pieces, -0.22, 0.18) * entries
    return jnp.clip(entries, min=-limit, max=limit).astype(held_as)


def setup_inputs(seed: int = 0) -> dict:
    arg_keys = jax.random.split(jax.random.key(seed), 9)
    node_rows = bell_draw(arg_keys[0], (NODES, D), 1.0, 6.0, ((0, 256),))
    w_self = bell_draw(arg_keys[1], (D, D), D ** -0.5, 0.1875)
    w_neigh = bell_draw(arg_keys[2], (D, D), D ** -0.5, 0.1875)
    hub_ids = draw_hub_ids(jax.random.fold_in(arg_keys[8], 71), 0)
    bnd_idx = draw_bnd_idx(jax.random.fold_in(arg_keys[8], 71), 0)
    send_pos = plant(jax.random.randint(arg_keys[5], (DEVICES, N_DEV, SLOT), 0, BND), jax.random.fold_in(arg_keys[5], 1), 0, BND - 1).astype(jnp.int32)
    edge_src = draw_edge_src(jax.random.fold_in(arg_keys[8], 71), 0)
    edge_dst = draw_edge_dst(jax.random.fold_in(arg_keys[8], 71), 0)
    return {"node_rows": node_rows, "w_self": w_self, "w_neigh": w_neigh, "hub_ids": hub_ids, "bnd_idx": bnd_idx, "send_pos": send_pos, "edge_src": edge_src, "edge_dst": edge_dst}


def reference(node_rows, w_self, w_neigh, hub_ids, bnd_idx, send_pos, edge_src, edge_dst):
    dev_count = NODES // NPD
    blocks = node_rows.reshape(dev_count, NPD, D)
    hub_rows = node_rows[hub_ids]
    src_all = edge_src.reshape(dev_count, E_DEV)
    dst_all = edge_dst.reshape(dev_count, E_DEV)

    def per_device(device):
        group_base = (device // N_DEV) * N_DEV
        peer_ids = group_base + jnp.arange(N_DEV, dtype=jnp.int32)
        positions = send_pos[peer_ids, device % N_DEV]
        local_rows = jnp.take_along_axis(bnd_idx[peer_ids], positions, axis=1)
        halo_rows = blocks[peer_ids[:, None], local_rows].reshape(N_DEV * SLOT, D)
        own_rows = blocks[device]
        row_table = jnp.concatenate([own_rows, halo_rows, hub_rows], axis=0)
        sources = src_all[device]
        targets = dst_all[device]
        gathered = row_table[sources].astype(jnp.float32)
        summed = jax.ops.segment_sum(gathered, targets, num_segments=NPD)
        degree = jax.ops.segment_sum(jnp.ones(sources.shape, jnp.float32), targets, num_segments=NPD)
        neighbour_mean = (summed / degree[:, None]).astype(jnp.bfloat16)
        mixed = jnp.dot(own_rows, w_self, preferred_element_type=jnp.float32)
        mixed = mixed + jnp.dot(neighbour_mean, w_neigh, preferred_element_type=jnp.float32)
        return jnp.maximum(mixed, 0.0).astype(jnp.bfloat16)

    result = lax.map(per_device, jnp.arange(dev_count, dtype=jnp.int32))
    return result.reshape(NODES, D)
```

```python
import jax
import jax.numpy as jnp
from jax import lax
from jax.experimental import pallas as pl
from jax.experimental.pallas import tpu as pltpu
from jax.sharding import PartitionSpec as P

D = 1024
NPD = 768
HUBS = 64
BND = 32
SLOT = 64
E_DEV = 6144
ROWS = E_DEV // 128
N_DEV = 32
N_GRP = 8
HALO = N_DEV * SLOT
STEP_ROWS = 12
STEP = STEP_ROWS * 128
COL = 256
DIGIT = 4096
MESH = pl.DeviceIdType.MESH
ONE_HOT = jnp.bfloat16
NT = (((1,), (1,)), ((), ()))
TN = (((0,), (0,)), ((), ()))


def kernel(node_hbm, ws_hbm, wn_hbm, hub_ids, bnd_idx, send_pos, edge_src, edge_dst,
           out_hbm,
           node, ws, wn, bnd, hubs, hmask, h1_recv, h2_out, h2_recv, sp_send, sp_recv,
           col_of, weight_of, one_dst, one_src, raw, halo_cnt, own_cnt, degree, acc, summed, mean, out_buf,
           in_sem, out_sem, blk_send, blk_recv, sib_send, sib_recv, small_send, small_recv):
    grp = lax.axis_index("grp")
    me = lax.axis_index("dev")
    x, y, c = me // 8, (me // 2) % 4, me % 2

    def at(dx, dy):
        return (((x + dx + 4) % 4) * 4 + (y + dy + 4) % 4) * 2 + c

    xm, xp, ym, yp = at(-1, 0), at(1, 0), at(0, -1), at(0, 1)
    sib = me + 1 - 2 * c

    node_in = pltpu.make_async_copy(node_hbm, node, in_sem.at[0])
    ws_in = pltpu.make_async_copy(ws_hbm, ws, in_sem.at[1])
    wn_in = pltpu.make_async_copy(wn_hbm, wn, in_sem.at[2])
    node_in.start()
    ws_in.start()
    wn_in.start()

    barrier = pltpu.get_barrier_semaphore()

    @pl.loop(1, N_DEV)
    def _(o):
        pl.semaphore_signal(barrier, inc=1, device_id=(grp, (me + o) % N_DEV), device_id_type=MESH)

    @pl.loop(1, N_GRP)
    def _(o):
        pl.semaphore_signal(barrier, inc=1, device_id=((grp + o) % N_GRP, me), device_id_type=MESH)

    for j in range(N_DEV):
        sp_send[j, 0:1, 0:SLOT] = send_pos[0, j : j + 1, :]

    node_in.wait()
    row_id = lax.broadcasted_iota(jnp.int32, (NPD, BND), 0)
    pick = jnp.where(row_id == bnd_idx[...], 1.0, 0.0).astype(jnp.bfloat16)
    rows = lax.dot_general(pick, node[...], TN, preferred_element_type=jnp.float32)
    bnd[pl.ds(pl.multiple_of(me * BND, BND), BND), :] = rows.astype(jnp.bfloat16)
    local = hub_ids[...] - (grp * N_DEV + me) * NPD
    row_id = lax.broadcasted_iota(jnp.int32, (NPD, HUBS), 0)
    pick = jnp.where(row_id == local, 1.0, 0.0).astype(jnp.bfloat16)
    rows = lax.dot_general(pick, node[...], TN, preferred_element_type=jnp.float32)
    hmask[...] = rows.astype(jnp.bfloat16)

    pl.semaphore_wait(barrier, N_DEV - 1 + N_GRP - 1)

    def piece(dev, lo, n, left, width):
        return bnd.at[pl.ds(pl.multiple_of(dev * BND + lo, 16), n), pl.ds(left, width)]

    def push(dev, to, phase, lo=0, n=BND, left=0, width=D):
        ref = piece(dev, lo, n, left, width)
        pltpu.make_async_remote_copy(ref, ref, blk_send, blk_recv.at[phase], device_id=(grp, to), device_id_type=MESH).start()

    def to_sib(dev, phase):
        ref = piece(dev, 0, BND, 0, D)
        pltpu.make_async_remote_copy(ref, ref, sib_send, sib_recv.at[phase], device_id=(grp, sib), device_id_type=MESH).start()

    def wait_rows(sem, n):
        ref = bnd.at[pl.ds(0, n), :]
        pltpu.make_async_copy(ref, ref, sem).wait()

    hub_row, hub_col = pl.multiple_of(16 * (me // 8), 16), pl.multiple_of(128 * (me % 8), 128)

    for to in (xm, xp, ym, yp):
        push(me, to, 0)

    @pl.loop(1, N_DEV)
    def _(o):
        to = (me + o) % N_DEV
        pltpu.make_async_remote_copy(sp_send.at[to], sp_recv.at[o - 1], small_send.at[0], small_recv.at[0],
                                     device_id=(grp, to), device_id_type=MESH).start()

    @pl.loop(1, N_DEV)
    def _(o):
        to = (me + o) % N_DEV
        src = hmask.at[pl.ds(pl.multiple_of(16 * (to // 8), 16), 16), pl.ds(pl.multiple_of(128 * (to % 8), 128), 128)]
        pltpu.make_async_remote_copy(src, h1_recv.at[o - 1], small_send.at[1], small_recv.at[1],
                                     device_id=(grp, to), device_id_type=MESH).start()

    to_sib(me, 0)
    sp_recv[N_DEV - 1] = sp_send[me]

    ws_in.wait()

    @pl.loop(0, D // COL)
    def _(i):
        cols = pl.ds(pl.multiple_of(i * COL, COL), COL)
        acc[:, cols] = jnp.dot(node[...], ws[:, cols], preferred_element_type=jnp.float32)

    wait_rows(blk_recv.at[0], 4 * BND)
    push(xm, xp, 1, 0, BND, 0, D // 2)
    push(xp, xm, 1, 0, BND, D // 2, D // 2)
    push(ym, yp, 1, 0, BND, 0, D // 2)
    push(yp, ym, 1, 0, BND, D // 2, D // 2)
    for from_x in (xm, xp):
        for to in (ym, yp):
            push(from_x, to, 1, 0, 16)
    for from_y in (ym, yp):
        for to in (xm, xp):
            push(from_y, to, 1, 16, 16)
    for dev in (xm, xp, ym, yp):
        to_sib(dev, 1)

    pltpu.make_async_copy(sp_recv.at[pl.ds(0, N_DEV - 1)], sp_recv.at[pl.ds(0, N_DEV - 1)], small_recv.at[0]).wait()
    src = edge_src[...]
    slot = src - NPD
    is_halo = jnp.logical_and(slot >= 0, slot < HALO)
    peer = jnp.where(is_halo, slot // SLOT, -1)
    within = jnp.where(is_halo, slot % SLOT, 0)
    weight_of[...] = jnp.where(is_halo, 1.0, float(DIGIT))
    col_of[...] = jnp.where(src >= NPD + HALO, src - HALO, src)

    @pl.loop(0, N_DEV)
    def _(j):
        table = jnp.broadcast_to(sp_recv[(me - j - 1 + N_DEV) % N_DEV], (ROWS, 128))
        found = jnp.take_along_axis(table, within, axis=1)
        col_of[...] = jnp.where(peer == j, found + j * BND, col_of[...])

    def count_step(step):
        @pl.loop(0, STEP_ROWS)
        def _(r):
            row = step * STEP_ROWS + r
            here = pl.ds(pl.multiple_of(r * 128, 128), 128)
            d = edge_dst[pl.ds(row, 1), :].astype(jnp.int16)
            s = col_of[pl.ds(row, 1), :].astype(jnp.int16)
            w = weight_of[pl.ds(row, 1), :].astype(jnp.bfloat16)
            zero = jnp.zeros((), jnp.bfloat16)
            one = jnp.ones((), jnp.bfloat16)
            id_d = lax.broadcasted_iota(jnp.int16, (NPD, 128), 0)
            one_dst[:, here] = jnp.where(id_d == d, one, zero).astype(ONE_HOT)
            id_s = lax.broadcasted_iota(jnp.int16, (D, 128), 0)
            one_src[:, here] = jnp.where(id_s == s, jnp.broadcast_to(w, (D, 128)), zero).astype(ONE_HOT)

        @pl.loop(0, D // COL)
        def _(i):
            cols = pl.ds(pl.multiple_of(i * COL, COL), COL)
            part = lax.dot_general(one_dst[...], one_src[cols, :], NT, preferred_element_type=jnp.float32)
            if step % 2 == 0:
                raw[step // 2, :, cols] = part
            else:
                raw[step // 2, :, cols] += part

    count_step(0)

    pltpu.make_async_copy(h1_recv, h1_recv, small_recv.at[1]).wait()
    block = jnp.sum(h1_recv[...].astype(jnp.float32), axis=0)
    block = block + hmask[pl.ds(hub_row, 16), pl.ds(hub_col, 128)].astype(jnp.float32)
    h2_out[0] = block.astype(jnp.bfloat16)

    @pl.loop(1, N_GRP)
    def _(o):
        pltpu.make_async_remote_copy(h2_out.at[0], h2_recv.at[o - 1], small_send.at[2], small_recv.at[2],
                                     device_id=((grp + o) % N_GRP, me), device_id_type=MESH).start()

    x2, y2 = at(2, 0), at(0, 2)
    mm, mp, pm, pp = at(-1, -1), at(-1, 1), at(1, -1), at(1, 1)
    wait_rows(blk_recv.at[1], 12 * 16)
    for to in (ym, yp):
        push(x2, to, 2, 0, 16)
    for to in (xm, xp):
        push(y2, to, 2, 16, 16)
    for dev in (mm, pm):
        push(dev, yp, 2, 0, 16, 0, D // 2)
    for dev in (mp, pp):
        push(dev, ym, 2, 0, 16, D // 2, D // 2)
    for dev in (mm, mp):
        push(dev, xp, 2, 16, 16, 0, D // 2)
    for dev in (pm, pp):
        push(dev, xm, 2, 16, 16, D // 2, D // 2)
    for dev in (x2, y2, mm, mp, pm, pp):
        to_sib(dev, 2)

    count_step(1)

    pltpu.make_async_copy(h2_recv, h2_recv, small_recv.at[2]).wait()
    block = jnp.sum(h2_recv[...].astype(jnp.float32), axis=0) + h2_out[0].astype(jnp.float32)
    mine = hubs.at[pl.ds(hub_row, 16), pl.ds(hub_col, 128)]
    mine[...] = block.astype(jnp.bfloat16)

    @pl.loop(1, N_DEV)
    def _(o):
        pltpu.make_async_remote_copy(mine, mine, small_send.at[3], small_recv.at[3],
                                     device_id=(grp, (me + o) % N_DEV), device_id_type=MESH).start()

    wait_rows(blk_recv.at[2], 8 * 16)
    x2m, x2p, m2, p2 = at(2, -1), at(2, 1), at(-1, 2), at(1, 2)
    push(x2m, yp, 3, 0, 16, 0, D // 2)
    push(x2p, ym, 3, 0, 16, D // 2, D // 2)
    push(m2, xp, 3, 16, 16, 0, D // 2)
    push(p2, xm, 3, 16, 16, D // 2, D // 2)
    for dev in (x2m, x2p, m2, p2):
        to_sib(dev, 3)

    count_step(2)

    wait_rows(blk_recv.at[3], BND)
    to_sib(at(2, 2), 4)

    count_step(3)

    degree[...] = jnp.zeros_like(degree)

    @pl.loop(0, D // COL)
    def _(i):
        cols = pl.ds(pl.multiple_of(i * COL, COL), COL)
        first, second = raw[0, :, cols], raw[1, :, cols]
        high_a, high_b = jnp.floor(first * (1.0 / DIGIT)), jnp.floor(second * (1.0 / DIGIT))
        high = high_a + high_b
        low = (first - high_a * DIGIT) + (second - high_b * DIGIT)
        own_cnt[:, cols] = high.astype(jnp.bfloat16)
        halo_cnt[:, cols] = low.astype(jnp.bfloat16)
        degree[...] += jnp.sum(high + low, axis=1, keepdims=True)

    @pl.loop(0, D // COL)
    def _(i):
        cols = pl.ds(pl.multiple_of(i * COL, COL), COL)
        summed[:, cols] = jnp.dot(own_cnt[:, 0:NPD], node[:, cols], preferred_element_type=jnp.float32)

    wait_rows(sib_recv.at[0], BND)
    wait_rows(sib_recv.at[1], 4 * BND)
    wait_rows(sib_recv.at[2], 6 * BND)
    wait_rows(sib_recv.at[3], 4 * BND)
    wait_rows(sib_recv.at[4], BND)
    pltpu.make_async_copy(h1_recv, h1_recv, small_recv.at[3]).wait()
    inverse = 1.0 / degree[...]

    @pl.loop(0, D // COL)
    def _(i):
        cols = pl.ds(pl.multiple_of(i * COL, COL), COL)
        total = summed[:, cols] + jnp.dot(halo_cnt[...], bnd[:, cols], preferred_element_type=jnp.float32)
        total = total + jnp.dot(own_cnt[:, NPD : NPD + HUBS], hubs[:, cols], preferred_element_type=jnp.float32)
        mean[:, cols] = (total * inverse).astype(jnp.bfloat16)

    wn_in.wait()

    @pl.loop(0, D // COL)
    def _(i):
        cols = pl.ds(pl.multiple_of(i * COL, COL), COL)
        mixed = acc[:, cols] + jnp.dot(mean[...], wn[:, cols], preferred_element_type=jnp.float32)
        out_buf[:, cols] = jnp.maximum(mixed, 0.0).astype(jnp.bfloat16)
        pltpu.make_async_copy(out_buf.at[:, cols], out_hbm.at[:, cols], out_sem).start()

    wait_rows(blk_send, 4 * BND + 12 * 16 + 8 * 16 + BND)
    wait_rows(sib_send, 16 * BND)
    pltpu.make_async_copy(sp_recv.at[pl.ds(0, N_DEV - 1)], sp_recv.at[pl.ds(0, N_DEV - 1)], small_send.at[0]).wait()
    pltpu.make_async_copy(h1_recv, h1_recv, small_send.at[1]).wait()
    pltpu.make_async_copy(h2_recv, h2_recv, small_send.at[2]).wait()
    pltpu.make_async_copy(h1_recv, h1_recv, small_send.at[3]).wait()
    pltpu.make_async_copy(out_buf, out_hbm, out_sem).wait()


def body(node_rows, w_self, w_neigh, hub_ids, bnd_idx, send_pos, edge_src, edge_dst):
    bf16, f32, i32 = jnp.bfloat16, jnp.float32, jnp.int32
    any_, vmem = pl.BlockSpec(memory_space=pl.ANY), pl.BlockSpec(memory_space=pltpu.VMEM)
    scratch = [
        pltpu.VMEM((NPD, D), bf16),
        pltpu.VMEM((D, D), bf16),
        pltpu.VMEM((D, D), bf16),
        pltpu.VMEM((N_DEV * BND, D), bf16),
        pltpu.VMEM((HUBS, D), bf16),
        pltpu.VMEM((HUBS, D), bf16),
        pltpu.VMEM((N_DEV - 1, 16, 128), bf16),
        pltpu.VMEM((1, 16, 128), bf16),
        pltpu.VMEM((N_GRP - 1, 16, 128), bf16),
        pltpu.VMEM((N_DEV, 1, 128), i32),
        pltpu.VMEM((N_DEV, 1, 128), i32),
        pltpu.VMEM((ROWS, 128), i32),
        pltpu.VMEM((ROWS, 128), f32),
        pltpu.VMEM((NPD, STEP), ONE_HOT),
        pltpu.VMEM((D, STEP), ONE_HOT),
        pltpu.VMEM((2, NPD, D), f32),
        pltpu.VMEM((NPD, D), bf16),
        pltpu.VMEM((NPD, D), bf16),
        pltpu.VMEM((NPD, 1), f32),
        pltpu.VMEM((NPD, D), f32),
        pltpu.VMEM((NPD, D), f32),
        pltpu.VMEM((NPD, D), bf16),
        pltpu.VMEM((NPD, D), bf16),
        pltpu.SemaphoreType.DMA((3,)),
        pltpu.SemaphoreType.DMA,
        pltpu.SemaphoreType.DMA,
        pltpu.SemaphoreType.DMA((4,)),
        pltpu.SemaphoreType.DMA,
        pltpu.SemaphoreType.DMA((5,)),
        pltpu.SemaphoreType.DMA((4,)),
        pltpu.SemaphoreType.DMA((4,)),
    ]
    return pl.pallas_call(
        kernel,
        out_shape=jax.ShapeDtypeStruct((NPD, D), bf16),
        in_specs=[any_, any_, any_, vmem, vmem, vmem, vmem, vmem],
        out_specs=any_,
        scratch_shapes=scratch,
        compiler_params=pltpu.CompilerParams(
            collective_id=0, has_side_effects=True, vmem_limit_bytes=56 * 2**20
        ),
        name="sage",
    )(
        node_rows, w_self, w_neigh, hub_ids.reshape(1, HUBS), bnd_idx, send_pos,
        edge_src.reshape(ROWS, 128), edge_dst.reshape(ROWS, 128),
    )


def solution(mesh):
    in_specs = (
        P(("grp", "dev"), None),
        P(),
        P(),
        P(),
        P(("grp", "dev"), None),
        P(("grp", "dev"), None, None),
        P(("grp", "dev")),
        P(("grp", "dev")),
    )
    out_specs = P(("grp", "dev"), None)
    return jax.shard_map(body, mesh=mesh, in_specs=in_specs, out_specs=out_specs, check_vma=False)
```

```python
import jax
import jax.numpy as jnp
from jax import lax
from jax.experimental import pallas as pl
from jax.experimental.pallas import tpu as pltpu
from jax.sharding import PartitionSpec as P

D = 1024
NPD = 768
HUBS = 64
BND = 32
SLOT = 64
E_DEV = 6144
ROWS = E_DEV // 128
N_DEV = 32
N_GRP = 8
HALO = N_DEV * SLOT
COLUMN = 2 * N_GRP
STEPS = 4
STEP_ROWS = ROWS // STEPS
STEP = STEP_ROWS * 128
HALO_DIGITS, HALO_BITS, HALO_LINES = 11, 2, 192
OWN_DIGITS, OWN_BITS, OWN_LINES, HUB_LINES = 8, 3, 96, 8
HUB_AT = HALO_LINES + OWN_LINES
DEGREE_AT = HUB_AT + HUB_LINES
LINES = DEGREE_AT + 8
LIMIT = 2.0**24
MESH = pl.DeviceIdType.MESH
NT = (((1,), (1,)), ((), ()))
TN = (((0,), (0,)), ((), ()))
BF16, F32, I32, I16 = jnp.bfloat16, jnp.float32, jnp.int32, jnp.int16


def dot(a, b, dims=(((1,), (0,)), ((), ()))):
    return lax.dot_general(a, b, dims, preferred_element_type=F32)


def place(dev, me):
    core = dev & 1
    dx = ((dev >> 3) - (me >> 3)) & 3
    dy = ((dev >> 1) - (me >> 1)) & 3
    du = jnp.where(core == 0, dx, dy)
    dv = jnp.where(core == 0, dy, dx)
    return 16 * (core ^ (me & 1)) + 4 * dv + du


def edge_column(src, me):
    slot = src - NPD
    is_halo = jnp.logical_and(slot >= 0, slot < HALO)
    halo = place((slot >> 6) & 31, me) * SLOT + (slot & 63)
    return jnp.where(is_halo, halo, jnp.where(src < NPD, src + HALO, src))


def hub_owner_rank(hub_ids):
    owner = hub_ids // NPD
    lines = lax.broadcasted_iota(I32, (N_DEV * N_GRP, HUBS), 0)
    member = jnp.where(lines == owner, 1.0, 0.0).astype(BF16)
    same = dot(member, member, TN)
    earlier = lax.broadcasted_iota(I32, (HUBS, HUBS), 0) < lax.broadcasted_iota(I32, (HUBS, HUBS), 1)
    rank = jnp.sum(jnp.where(earlier, same, 0.0), axis=0, keepdims=True)
    return owner, rank.astype(I32)


def main_kernel(node_hbm, ws_hbm, wn_hbm, hub_ids, bnd_idx, send_pos, edge_src, edge_dst,
                out_hbm, bnd_hbm, hubs_hbm, remap_hbm, flag,
                node, ws, wn, bnd, pos, column, hubs, tile_z, remap,
                line_of, weight_of, one_dst_a, one_dst_b, one_src_a, one_src_b, packed,
                halo_cnt, own_cnt, bnd_cnt, acc, summed, out_buf,
                in_sem, out_sem, b_send, b_sib_send, p_send, p_sib_send, h_send, h_sib_send, z_send, recv):
    grp = lax.axis_index("grp")
    me = lax.axis_index("dev")
    x, y, c = me // 8, (me // 2) % 4, me % 2
    sib = me + 1 - 2 * c

    def at(du, dv):
        dx, dy = du * (1 - c) + dv * c, dv * (1 - c) + du * c
        return (((x + dx) % 4) * 4 + (y + dy) % 4) * 2 + c

    node_in = pltpu.make_async_copy(node_hbm, node, in_sem.at[0])
    ws_in = pltpu.make_async_copy(ws_hbm, ws, in_sem.at[1])
    wn_in = pltpu.make_async_copy(wn_hbm, wn, in_sem.at[2])
    node_in.start()
    ws_in.start()
    wn_in.start()

    barrier = pltpu.get_barrier_semaphore()
    for near in [at(1, 0), at(3, 0), at(2, 0), at(0, 1), at(0, 3), at(0, 2), sib]:
        pl.semaphore_signal(barrier, inc=1, device_id=(grp, near), device_id_type=MESH)
    for o in range(1, N_GRP):
        pl.semaphore_signal(barrier, inc=1, device_id=((grp + o) % N_GRP, me), device_id_type=MESH)

    def copy(src, dst, send, got, g, to):
        pltpu.make_async_remote_copy(src, dst, send, recv.at[got], device_id=(g, to), device_id_type=MESH).start()

    def blocks(ref, n, lo, count):
        return ref.at[pl.ds(lo * n, count * n), :]

    def spread_u(ref, n, send, got):
        for du in (1, 3, 2):
            copy(blocks(ref, n, 0, 1), blocks(ref, n, 4 - du, 1), send, got, grp, at(du, 0))

    def spread_v(ref, n, lo, count, send, got):
        for dv in (1, 3, 2):
            copy(blocks(ref, n, lo, count), blocks(ref, n, 4 * (4 - dv) + lo, count), send, got, grp, at(0, dv))

    def spread_sib(ref, n, lo, count, send, got):
        copy(blocks(ref, n, lo, count), blocks(ref, n, 16 + lo, count), send, got, grp, sib)

    def done(ref, n, count, sem):
        part = blocks(ref, n, 0, count)
        pltpu.make_async_copy(part, part, sem).wait()

    positions = send_pos[0].astype(F32)
    pos[0:16, 0:SLOT] = positions[0:16].astype(BF16)
    pos[0:16, SLOT:128] = positions[16:32].astype(BF16)
    owner, rank = hub_owner_rank(hub_ids[...])
    local = hub_ids[...] - (grp * N_DEV + me) * NPD
    node_in.wait()
    pick = jnp.where(lax.broadcasted_iota(I32, (NPD, BND), 0) == bnd_idx[...], 1.0, 0.0).astype(BF16)
    bnd[0:BND, :] = dot(pick, node[...], TN).astype(BF16)
    pick = jnp.where(lax.broadcasted_iota(I32, (NPD, HUBS), 0) == local, 1.0, 0.0).astype(BF16)
    rows = dot(pick, node[...], TN).astype(BF16)
    by_rank = jnp.where(lax.broadcasted_iota(I32, (8, HUBS), 0) == rank, 1.0, 0.0).astype(BF16)
    pair = dot(by_rank, rows)
    tile = jnp.concatenate([pair[0:2, q * 128 : (q + 1) * 128] for q in range(8)], axis=0)
    tile_z[0] = tile.astype(BF16)

    pl.semaphore_wait(barrier, 7 + N_GRP - 1)

    spread_u(bnd, BND, b_send, 0)
    spread_u(pos, 16, p_send, 1)
    for o in range(1, N_GRP):
        copy(tile_z.at[0], tile_z.at[o], z_send, 2, (grp + o) % N_GRP, me)
    spread_sib(bnd, BND, 0, 1, b_sib_send, 3)

    col = edge_column(edge_src[...], me)
    third = lambda n: (n * 43) >> 7
    own = col - HALO
    hub = own - NPD
    halo_digit, own_digit = third(col >> 6), third(own >> 5)
    line = jnp.where(own < 0, col - HALO_LINES * halo_digit,
                     jnp.where(hub < 0, HALO_LINES + own - OWN_LINES * own_digit, HUB_AT + (hub & 7)))
    shift = jnp.where(own < 0, HALO_BITS * halo_digit, OWN_BITS * jnp.where(hub < 0, own_digit, hub >> 3))
    line_of[...] = line
    weight_of[...] = jnp.left_shift(jnp.ones_like(shift), shift).astype(F32)

    def make(step):
        one_dst, one_src = ((one_dst_a, one_src_a), (one_dst_b, one_src_b))[step % 2]
        zero, one = jnp.zeros((), BF16), jnp.ones((), BF16)
        for r in range(STEP_ROWS):
            row = step * STEP_ROWS + r
            here = slice(r * 128, (r + 1) * 128)
            d = edge_dst[row : row + 1, :].astype(I16)
            s = line_of[row : row + 1, :].astype(I16)
            w = weight_of[row : row + 1, :].astype(BF16)
            one_dst[:, here] = jnp.where(lax.broadcasted_iota(I16, (NPD, 128), 0) == d, one, zero)
            lines = lax.broadcasted_iota(I16, (LINES, 128), 0)
            value = jnp.where(lines == s, jnp.broadcast_to(w, (LINES, 128)), zero)
            one_src[:, here] = jnp.where(lines >= DEGREE_AT, one, value)

    def add(step):
        one_dst, one_src = ((one_dst_a, one_src_a), (one_dst_b, one_src_b))[step % 2]
        part = dot(one_src[...], one_dst[...], NT)
        packed[...] = part if step == 0 else packed[...] + part

    make(0)
    spread_v(bnd, BND, 0, 1, b_send, 4)
    make(1)
    add(0)

    done(bnd, BND, 3, recv.at[0])
    spread_v(bnd, BND, 1, 3, b_send, 5)
    spread_sib(bnd, BND, 1, 3, b_sib_send, 3)
    done(pos, 16, 3, recv.at[1])
    spread_v(pos, 16, 0, 4, p_send, 6)
    part = tile_z.at[pl.ds(1, N_GRP - 1)]
    pltpu.make_async_copy(part, part, recv.at[2]).wait()
    tiles = [tile_z[o].astype(F32) for o in range(N_GRP)]
    for q in range(8):
        rows = jnp.concatenate([t[2 * q : 2 * q + 2, :] for t in tiles], axis=0)
        column[0:COLUMN, q * 128 : (q + 1) * 128] = rows.astype(BF16)
    spread_u(column, COLUMN, h_send, 7)

    make(2)
    add(1)
    make(3)
    add(2)
    add(3)

    done(column, COLUMN, 3, recv.at[7])
    spread_v(column, COLUMN, 0, 4, h_send, 8)
    spread_sib(column, COLUMN, 0, 4, h_sib_send, 9)
    done(pos, 16, 12, recv.at[6])
    spread_sib(pos, 16, 0, 16, p_sib_send, 10)

    total = jnp.zeros((1, NPD), I32)
    ints = packed[0:HALO_LINES, :].astype(I32)
    for i in range(HALO_DIGITS):
        digit = ints >> (HALO_BITS * i)
        if i < HALO_DIGITS - 1:
            digit = digit & (2**HALO_BITS - 1)
        total = total + jnp.sum(digit, axis=0, keepdims=True)
        halo_cnt[i * HALO_LINES : (i + 1) * HALO_LINES, :] = digit.astype(F32).astype(BF16)
    ints = packed[HALO_LINES:DEGREE_AT, :].astype(I32)
    hub_parts = []
    for i in range(OWN_DIGITS):
        digit = ints >> (OWN_BITS * i)
        if i < OWN_DIGITS - 1:
            digit = digit & (2**OWN_BITS - 1)
        total = total + jnp.sum(digit, axis=0, keepdims=True)
        digit = digit.astype(F32)
        own_cnt[i * OWN_LINES : (i + 1) * OWN_LINES, :] = digit[0:OWN_LINES].astype(BF16)
        hub_parts.append(digit[OWN_LINES:])
    own_cnt[NPD : NPD + HUBS, :] = jnp.concatenate(hub_parts, axis=0).astype(BF16)
    degree = packed[DEGREE_AT : DEGREE_AT + 1, :]
    largest = jnp.max(packed[0:DEGREE_AT, :], axis=0, keepdims=True)
    bad = (total != degree.astype(I32)) | (largest >= LIMIT) | (degree > 256.0)
    flag[...] = jnp.broadcast_to(jnp.max(jnp.where(bad, 1, 0), axis=1, keepdims=True), (8, 128))
    inverse = jnp.transpose(jnp.broadcast_to(1.0 / degree, (128, NPD)))
    inverse = jnp.concatenate([inverse] * 8, axis=1)

    def third_of(i):
        return slice(i * 256, (i + 1) * 256)

    ws_in.wait()
    for i in range(3):
        acc[third_of(i), :] = dot(node[third_of(i), :], ws[...])

    done(bnd, BND, 3, recv.at[4])
    done(bnd, BND, 9, recv.at[5])
    spread_sib(bnd, BND, 4, 12, b_sib_send, 11)

    for i in range(3):
        summed[third_of(i), :] = dot(own_cnt[0:NPD, third_of(i)], node[...], TN)

    done(column, COLUMN, 12, recv.at[8])
    spread_sib(column, COLUMN, 4, 12, h_sib_send, 9)

    done(pos, 16, 16, recv.at[10])
    every = pos[...].astype(F32).reshape(N_DEV, 16, 128)
    mine = lax.broadcasted_iota(I32, (N_DEV, 16, 128), 1) == me % 16
    rows = jnp.sum(jnp.where(mine, every, 0.0), axis=1)
    turned = pltpu.roll(rows, SLOT, 1)
    low = jnp.where(me < 16, rows, turned)
    high = jnp.where(me < 16, turned, rows)
    lane = lax.broadcasted_iota(I32, (128, 128), 1)
    line = lax.broadcasted_iota(I32, (128, 128), 0)
    for g in range(8):
        for half in range(2):
            a = 4 * g + 2 * half
            wanted = jnp.where(lane < SLOT, low[a : a + 1, :], high[a + 1 : a + 2, :]).astype(I32)
            match = ((line >> 5) == 2 * half + (lane >> 6)) & ((line & 31) == wanted)
            remap[g * 128 : (g + 1) * 128, half * 128 : (half + 1) * 128] = jnp.where(match, 1.0, 0.0).astype(BF16)
    for g in range(8):
        part = dot(remap[g * 128 : (g + 1) * 128, :], halo_cnt[g * 256 : (g + 1) * 256, :])
        bnd_cnt[g * 128 : (g + 1) * 128, :] = part.astype(BF16)

    done(bnd, BND, 4, recv.at[3])
    done(bnd, BND, 12, recv.at[11])
    bnd_out = pltpu.make_async_copy(bnd, bnd_hbm, out_sem.at[0])
    bnd_out.start()
    for i in range(3):
        summed[third_of(i), :] += dot(bnd_cnt[:, third_of(i)], bnd[...], TN)

    done(column, COLUMN, 16, recv.at[9])
    at_row = place(owner % N_DEV, me) * COLUMN + ((grp - owner // N_DEV) & 7) * 2 + rank
    choose = jnp.where(lax.broadcasted_iota(I32, (N_DEV * COLUMN, HUBS), 0) == at_row, 1.0, 0.0).astype(BF16)
    hubs[...] = dot(choose, column[...], TN).astype(BF16)
    hubs_out = pltpu.make_async_copy(hubs, hubs_hbm, out_sem.at[1])
    hubs_out.start()
    remap_out = pltpu.make_async_copy(remap, remap_hbm, out_sem.at[2])
    remap_out.start()

    wn_in.wait()
    for i in range(3):
        total = summed[third_of(i), :] + dot(own_cnt[NPD : NPD + HUBS, third_of(i)], hubs[...], TN)
        mean = (total * inverse[third_of(i), :]).astype(BF16)
        mixed = acc[third_of(i), :] + dot(mean, wn[...])
        out_buf[third_of(i), :] = jnp.maximum(mixed, 0.0).astype(BF16)
        pltpu.make_async_copy(out_buf.at[third_of(i), :], out_hbm.at[third_of(i), :], out_sem.at[3]).start()

    done(bnd, BND, 15, b_send)
    done(bnd, BND, 16, b_sib_send)
    done(pos, 16, 15, p_send)
    done(pos, 16, 16, p_sib_send)
    done(column, COLUMN, 15, h_send)
    done(column, COLUMN, 16, h_sib_send)
    part = tile_z.at[pl.ds(1, N_GRP - 1)]
    pltpu.make_async_copy(part, part, z_send).wait()
    bnd_out.wait()
    hubs_out.wait()
    remap_out.wait()
    pltpu.make_async_copy(out_buf, out_hbm, out_sem.at[3]).wait()


def finish_kernel(flag, fast_hbm, node_hbm, ws_hbm, wn_hbm, bnd_hbm, hubs_hbm, remap_hbm, edge_src, edge_dst,
                  out_hbm,
                  node, ws, wn, bnd, hubs, remap, one_dst, one_src, col_of, summed, degree, out_buf, sem):
    me = lax.axis_index("dev")

    @pl.when(flag[0, 0] == 0)
    def _():
        parts = [pl.ds(i * 192, 192) for i in range(4)]
        ins = [pltpu.make_async_copy(fast_hbm.at[p, :], out_buf.at[p, :], sem.at[i]) for i, p in enumerate(parts)]
        outs = [pltpu.make_async_copy(out_buf.at[p, :], out_hbm.at[p, :], sem.at[4 + i]) for i, p in enumerate(parts)]
        for one in ins:
            one.start()
        for one, two in zip(ins, outs):
            one.wait()
            two.start()
        for two in outs:
            two.wait()

    @pl.when(flag[0, 0] != 0)
    def _():
        pairs = [(node_hbm, node), (ws_hbm, ws), (wn_hbm, wn), (bnd_hbm, bnd), (hubs_hbm, hubs), (remap_hbm, remap)]
        copies = [pltpu.make_async_copy(a, b, sem.at[i]) for i, (a, b) in enumerate(pairs)]
        for one in copies:
            one.start()
        for one in copies:
            one.wait()
        col_of[...] = edge_column(edge_src[...], me)
        degree[...] = jnp.zeros_like(degree)
        summed[...] = jnp.zeros_like(summed)

        @pl.loop(0, ROWS)
        def _(r):
            here = pl.ds(pl.multiple_of(r * 128, 128), 128)
            match = lax.broadcasted_iota(I32, (NPD, 128), 0) == edge_dst[pl.ds(r, 1), :]
            hit = jnp.where(match, 1.0, 0.0)
            one_dst[:, here] = hit.astype(BF16)
            degree[...] += jnp.sum(hit, axis=1, keepdims=True)

        def block(first, rows):
            n = rows.shape[0]

            @pl.loop(0, ROWS)
            def _(r):
                here = pl.ds(pl.multiple_of(r * 128, 128), 128)
                match = lax.broadcasted_iota(I32, (256, 128), 0) + first == col_of[pl.ds(r, 1), :]
                one_src[:, here] = jnp.where(match, 1.0, 0.0).astype(BF16)

            count = jnp.zeros((NPD, 256), F32)
            for i in range(STEPS):
                here = slice(i * STEP, (i + 1) * STEP)
                count = count + dot(one_dst[:, here], one_src[:, here], NT)
            upper = jnp.floor(count * (1.0 / 256.0)) * 256.0
            lower = count - upper
            summed[...] += dot(upper[:, 0:n].astype(BF16), rows) + dot(lower[:, 0:n].astype(BF16), rows)

        @pl.loop(0, 8)
        def _(g):
            lines = pl.ds(pl.multiple_of(g * 128, 128), 128)
            block(g * 256, dot(remap[lines, :], bnd[lines, :], TN).astype(BF16))

        @pl.loop(0, 3)
        def _(g):
            block(HALO + g * 256, node[pl.ds(pl.multiple_of(g * 256, 256), 256), :])

        block(HALO + NPD, hubs[...])
        mean = (summed[...] / degree[...]).astype(BF16)
        mixed = dot(node[...], ws[...]) + dot(mean, wn[...])
        out_buf[...] = jnp.maximum(mixed, 0.0).astype(BF16)
        last = pltpu.make_async_copy(out_buf, out_hbm, sem.at[0])
        last.start()
        last.wait()


def body(node_rows, w_self, w_neigh, hub_ids, bnd_idx, send_pos, edge_src, edge_dst):
    any_, vmem = pl.BlockSpec(memory_space=pl.ANY), pl.BlockSpec(memory_space=pltpu.VMEM)
    dma = pltpu.SemaphoreType.DMA
    src, dst = edge_src.reshape(ROWS, 128), edge_dst.reshape(ROWS, 128)
    scratch = [
        pltpu.VMEM((NPD, D), BF16),
        pltpu.VMEM((D, D), BF16),
        pltpu.VMEM((D, D), BF16),
        pltpu.VMEM((N_DEV * BND, D), BF16),
        pltpu.VMEM((N_DEV * 16, 128), BF16),
        pltpu.VMEM((N_DEV * COLUMN, D), BF16),
        pltpu.VMEM((HUBS, D), BF16),
        pltpu.VMEM((N_GRP, 16, 128), BF16),
        pltpu.VMEM((N_DEV * BND, 256), BF16),
        pltpu.VMEM((ROWS, 128), I32),
        pltpu.VMEM((ROWS, 128), F32),
        pltpu.VMEM((NPD, STEP), BF16),
        pltpu.VMEM((NPD, STEP), BF16),
        pltpu.VMEM((LINES, STEP), BF16),
        pltpu.VMEM((LINES, STEP), BF16),
        pltpu.VMEM((LINES, NPD), F32),
        pltpu.VMEM((HALO_DIGITS * HALO_LINES, NPD), BF16),
        pltpu.VMEM((NPD + HUBS, NPD), BF16),
        pltpu.VMEM((N_DEV * BND, NPD), BF16),
        pltpu.VMEM((NPD, D), F32),
        pltpu.VMEM((NPD, D), F32),
        pltpu.VMEM((NPD, D), BF16),
        dma((3,)), dma((4,)), dma, dma, dma, dma, dma, dma, dma, dma((12,)),
    ]
    outs = [
        jax.ShapeDtypeStruct((NPD, D), BF16),
        jax.ShapeDtypeStruct((N_DEV * BND, D), BF16),
        jax.ShapeDtypeStruct((HUBS, D), BF16),
        jax.ShapeDtypeStruct((N_DEV * BND, 256), BF16),
        jax.ShapeDtypeStruct((8, 128), I32),
    ]
    fast, bnd, hubs, remap, flag = pl.pallas_call(
        main_kernel,
        out_shape=outs,
        in_specs=[any_, any_, any_, vmem, vmem, vmem, vmem, vmem],
        out_specs=[any_, any_, any_, any_, vmem],
        scratch_shapes=scratch,
        compiler_params=pltpu.CompilerParams(
            collective_id=0, has_side_effects=True, vmem_limit_bytes=56 * 2**20
        ),
        name="sage_main",
    )(node_rows, w_self, w_neigh, hub_ids.reshape(1, HUBS), bnd_idx, send_pos, src, dst)
    scratch = [
        pltpu.VMEM((NPD, D), BF16),
        pltpu.VMEM((D, D), BF16),
        pltpu.VMEM((D, D), BF16),
        pltpu.VMEM((N_DEV * BND, D), BF16),
        pltpu.VMEM((HUBS, D), BF16),
        pltpu.VMEM((N_DEV * BND, 256), BF16),
        pltpu.VMEM((NPD, E_DEV), BF16),
        pltpu.VMEM((256, E_DEV), BF16),
        pltpu.VMEM((ROWS, 128), I32),
        pltpu.VMEM((NPD, D), F32),
        pltpu.VMEM((NPD, 1), F32),
        pltpu.VMEM((NPD, D), BF16),
        dma((8,)),
    ]
    return pl.pallas_call(
        finish_kernel,
        out_shape=jax.ShapeDtypeStruct((NPD, D), BF16),
        in_specs=[pl.BlockSpec(memory_space=pltpu.SMEM)] + [any_] * 7 + [vmem, vmem],
        out_specs=any_,
        scratch_shapes=scratch,
        compiler_params=pltpu.CompilerParams(vmem_limit_bytes=56 * 2**20),
        name="sage_finish",
    )(flag, fast, node_rows, w_self, w_neigh, bnd, hubs, remap, src, dst)


def solution(mesh):
    in_specs = (
        P(("grp", "dev"), None),
        P(),
        P(),
        P(),
        P(("grp", "dev"), None),
        P(("grp", "dev"), None, None),
        P(("grp", "dev")),
        P(("grp", "dev")),
    )
    out_specs = P(("grp", "dev"), None)
    return jax.shard_map(body, mesh=mesh, in_specs=in_specs, out_specs=out_specs, check_vma=False)
```

```python
import jax
import jax.numpy as jnp
from jax import lax
from jax.experimental import pallas as pl
from jax.experimental.pallas import tpu as pltpu
from jax.sharding import PartitionSpec as P

D = 1024
NPD = 768
HUBS = 64
BND = 32
SLOT = 64
E_DEV = 6144
ROWS = E_DEV // 128
N_DEV = 32
N_GRP = 8
HALO = N_DEV * SLOT
COLUMN = 2 * N_GRP
STEPS = 4
STEP_ROWS = ROWS // STEPS
STEP = STEP_ROWS * 128
HALO_DIGITS, HALO_BITS, HALO_LINES = 11, 2, 192
OWN_DIGITS, OWN_BITS, OWN_LINES, HUB_LINES = 8, 3, 96, 8
HUB_AT = HALO_LINES + OWN_LINES
DEGREE_AT = HUB_AT + HUB_LINES
LINES = DEGREE_AT + 8
LIMIT = 2.0**24
MESH = pl.DeviceIdType.MESH
NT = (((1,), (1,)), ((), ()))
TN = (((0,), (0,)), ((), ()))
BF16, F32, I32, I16 = jnp.bfloat16, jnp.float32, jnp.int32, jnp.int16


def dot(a, b, dims=(((1,), (0,)), ((), ()))):
    return lax.dot_general(a, b, dims, preferred_element_type=F32)


def place(dev, me):
    core = dev & 1
    dx = ((dev >> 3) - (me >> 3)) & 3
    dy = ((dev >> 1) - (me >> 1)) & 3
    du = jnp.where(core == 0, dx, dy)
    dv = jnp.where(core == 0, dy, dx)
    return 16 * (core ^ (me & 1)) + 4 * dv + du


def edge_column(src, me):
    slot = src - NPD
    is_halo = jnp.logical_and(slot >= 0, slot < HALO)
    halo = place((slot >> 6) & 31, me) * SLOT + (slot & 63)
    return jnp.where(is_halo, halo, jnp.where(src < NPD, src + HALO, src))


def hub_owner_rank(hub_ids):
    owner = hub_ids // NPD
    lines = lax.broadcasted_iota(I32, (N_DEV * N_GRP, HUBS), 0)
    member = jnp.where(lines == owner, 1.0, 0.0).astype(BF16)
    same = dot(member, member, TN)
    earlier = lax.broadcasted_iota(I32, (HUBS, HUBS), 0) < lax.broadcasted_iota(I32, (HUBS, HUBS), 1)
    rank = jnp.sum(jnp.where(earlier, same, 0.0), axis=0, keepdims=True)
    return owner, rank.astype(I32)


def main_kernel(node_hbm, ws_hbm, wn_hbm, hub_ids, bnd_idx, send_pos, edge_src, edge_dst,
                out_hbm, bnd_hbm, column_hbm, remap_hbm, flag,
                node, ws, wn, bnd, pos, column, tile_z, remap,
                line_of, weight_of, one_dst, one_src, packed, inverse,
                halo_cnt, own_cnt, hub_cnt, column_cnt, bnd_cnt, acc, summed, out_buf,
                in_sem, out_sem, b_send, b_sib_send, p_send, p_sib_send, h_send, h_sib_send, z_send, recv):
    grp = lax.axis_index("grp")
    me = lax.axis_index("dev")
    x, y, c = me // 8, (me // 2) % 4, me % 2
    sib = me + 1 - 2 * c

    def at(du, dv):
        dx, dy = du * (1 - c) + dv * c, dv * (1 - c) + du * c
        return (((x + dx) % 4) * 4 + (y + dy) % 4) * 2 + c

    node_in = pltpu.make_async_copy(node_hbm, node, in_sem.at[0])
    ws_in = pltpu.make_async_copy(ws_hbm, ws, in_sem.at[1])
    wn_in = pltpu.make_async_copy(wn_hbm, wn, in_sem.at[2])
    node_in.start()
    ws_in.start()
    wn_in.start()

    barrier = pltpu.get_barrier_semaphore()
    for near in [at(1, 0), at(3, 0), at(2, 0), at(0, 1), at(0, 3), at(0, 2), sib]:
        pl.semaphore_signal(barrier, inc=1, device_id=(grp, near), device_id_type=MESH)
    for o in range(1, N_GRP):
        pl.semaphore_signal(barrier, inc=1, device_id=((grp + o) % N_GRP, me), device_id_type=MESH)

    packed[...] = jnp.zeros_like(packed)

    def copy(src, dst, send, got, g, to):
        pltpu.make_async_remote_copy(src, dst, send, recv.at[got], device_id=(g, to), device_id_type=MESH).start()

    def blocks(ref, n, lo, count):
        return ref.at[pl.ds(lo * n, count * n), :]

    def spread_u(ref, n, send, got):
        for du in (1, 3, 2):
            copy(blocks(ref, n, 0, 1), blocks(ref, n, 4 - du, 1), send, got, grp, at(du, 0))

    def spread_v(ref, n, lo, count, send, got):
        for dv in (1, 3, 2):
            copy(blocks(ref, n, lo, count), blocks(ref, n, 4 * (4 - dv) + lo, count), send, got, grp, at(0, dv))

    def spread_sib(ref, n, lo, count, send, got):
        copy(blocks(ref, n, lo, count), blocks(ref, n, 16 + lo, count), send, got, grp, sib)

    def done(ref, n, count, sem):
        part = blocks(ref, n, 0, count)
        pltpu.make_async_copy(part, part, sem).wait()

    owner, rank = hub_owner_rank(hub_ids[...])
    local = hub_ids[...] - (grp * N_DEV + me) * NPD
    wanted = jnp.concatenate([local, bnd_idx[...]], axis=1)
    pick = jnp.where(lax.broadcasted_iota(I32, (NPD, HUBS + BND), 0) == wanted, 1.0, 0.0).astype(BF16)
    by_rank = jnp.where(lax.broadcasted_iota(I32, (8, HUBS), 0) == rank, 1.0, 0.0).astype(BF16)
    positions = send_pos[0].astype(F32)
    pos[0:16, 0:SLOT] = positions[0:16].astype(BF16)
    pos[0:16, SLOT:128] = positions[16:32].astype(BF16)
    node_in.wait()
    rows = dot(pick, node[...], TN).astype(BF16)
    bnd[0:BND, :] = rows[HUBS:]
    pair = dot(by_rank, rows[0:HUBS])
    tile = jnp.concatenate([pair[0:2, q * 128 : (q + 1) * 128] for q in range(8)], axis=0)
    tile_z[0] = tile.astype(BF16)

    col = edge_column(edge_src[...], me)
    third = lambda n: (n * 43) >> 7
    own = col - HALO
    hub = own - NPD
    halo_digit, own_digit = third(col >> 6), third(own >> 5)
    line = jnp.where(own < 0, col - HALO_LINES * halo_digit,
                     jnp.where(hub < 0, HALO_LINES + own - OWN_LINES * own_digit, HUB_AT + (hub & 7)))
    shift = jnp.where(own < 0, HALO_BITS * halo_digit, OWN_BITS * jnp.where(hub < 0, own_digit, hub >> 3))
    line_of[...] = line
    weight_of[...] = jnp.left_shift(jnp.ones_like(shift), shift).astype(F32)

    distance = jnp.minimum(grp, N_GRP - grp)
    first_send = jnp.maximum(2 - distance, 0)

    @pl.loop(0, STEPS)
    def _(step):
        @pl.when(step == first_send)
        def _():
            pl.semaphore_wait(barrier, 7 + N_GRP - 1)
            for o in range(1, N_GRP):
                copy(tile_z.at[0], tile_z.at[o], z_send, 2, (grp + o) % N_GRP, me)
            spread_u(bnd, BND, b_send, 0)
            spread_u(pos, 16, p_send, 1)
            spread_sib(bnd, BND, 0, 1, b_sib_send, 3)

        zero, one = jnp.zeros((), BF16), jnp.ones((), BF16)
        for r in range(STEP_ROWS):
            row = pl.ds(step * STEP_ROWS + r, 1)
            here = slice(r * 128, (r + 1) * 128)
            d = edge_dst[row, :].astype(I16)
            s = line_of[row, :].astype(I16)
            w = weight_of[row, :].astype(BF16)
            one_dst[:, here] = jnp.where(lax.broadcasted_iota(I16, (NPD, 128), 0) == d, one, zero)
            lines = lax.broadcasted_iota(I16, (LINES, 128), 0)
            value = jnp.where(lines == s, jnp.broadcast_to(w, (LINES, 128)), zero)
            one_src[:, here] = jnp.where(lines >= DEGREE_AT, one, value)
        packed[...] += dot(one_src[...], one_dst[...], NT)

        @pl.when(step == first_send)
        def _():
            spread_v(bnd, BND, 0, 1, b_send, 4)

    total = jnp.zeros((1, NPD), I32)
    ints = packed[0:HALO_LINES, :].astype(I32)
    for i in range(HALO_DIGITS):
        digit = ints >> (HALO_BITS * i)
        if i < HALO_DIGITS - 1:
            digit = digit & (2**HALO_BITS - 1)
        total = total + jnp.sum(digit, axis=0, keepdims=True)
        halo_cnt[i * HALO_LINES : (i + 1) * HALO_LINES, :] = digit.astype(F32).astype(BF16)
    ints = packed[HALO_LINES:DEGREE_AT, :].astype(I32)
    hub_parts = []
    for i in range(OWN_DIGITS):
        digit = ints >> (OWN_BITS * i)
        if i < OWN_DIGITS - 1:
            digit = digit & (2**OWN_BITS - 1)
        total = total + jnp.sum(digit, axis=0, keepdims=True)
        digit = digit.astype(F32)
        own_cnt[i * OWN_LINES : (i + 1) * OWN_LINES, :] = digit[0:OWN_LINES].astype(BF16)
        hub_parts.append(digit[OWN_LINES:])
    hub_cnt[...] = jnp.concatenate(hub_parts, axis=0).astype(BF16)

    degree = packed[DEGREE_AT : DEGREE_AT + 1, :]
    largest = jnp.max(packed[0:DEGREE_AT, :], axis=0, keepdims=True)
    bad = (total != degree.astype(I32)) | (largest >= LIMIT) | (degree > 256.0)
    flag[...] = jnp.broadcast_to(jnp.max(jnp.where(bad, 1, 0), axis=1, keepdims=True), (8, 128))
    inverse[...] = jnp.transpose(jnp.broadcast_to(1.0 / degree, (128, NPD)))

    def third_of(i):
        return slice(i * 256, (i + 1) * 256)

    done(bnd, BND, 3, recv.at[0])
    spread_v(bnd, BND, 1, 3, b_send, 5)
    done(pos, 16, 3, recv.at[1])
    spread_v(pos, 16, 0, 4, p_send, 6)
    spread_sib(bnd, BND, 1, 3, b_sib_send, 3)

    ws_in.wait()
    for i in range(3):
        acc[third_of(i), :] = dot(node[third_of(i), :], ws[...])

    for i in range(3):
        summed[third_of(i), :] = dot(own_cnt[0:NPD, third_of(i)], node[...], TN)

    part = tile_z.at[pl.ds(1, N_GRP - 1)]
    pltpu.make_async_copy(part, part, recv.at[2]).wait()
    tiles = [tile_z[o].astype(F32) for o in range(N_GRP)]
    for q in range(8):
        rows = jnp.concatenate([t[2 * q : 2 * q + 2, :] for t in tiles], axis=0)
        column[0:COLUMN, q * 128 : (q + 1) * 128] = rows.astype(BF16)
    spread_u(column, COLUMN, h_send, 7)

    done(pos, 16, 12, recv.at[6])
    spread_sib(pos, 16, 0, 16, p_sib_send, 10)

    at_row = place(owner % N_DEV, me) * COLUMN + ((grp - owner // N_DEV) & 7) * 2 + rank
    choose = jnp.where(lax.broadcasted_iota(I32, (N_DEV * COLUMN, HUBS), 0) == at_row, 1.0, 0.0).astype(BF16)
    column_cnt[...] = dot(choose, hub_cnt[...]).astype(BF16)

    done(column, COLUMN, 3, recv.at[7])
    spread_v(column, COLUMN, 0, 4, h_send, 8)
    spread_sib(column, COLUMN, 0, 4, h_sib_send, 9)

    done(pos, 16, 16, recv.at[10])
    every = pos[...].astype(F32).reshape(N_DEV, 16, 128)
    mine = lax.broadcasted_iota(I32, (N_DEV, 16, 128), 1) == me % 16
    rows = jnp.sum(jnp.where(mine, every, 0.0), axis=1)
    turned = pltpu.roll(rows, SLOT, 1)
    low = jnp.where(me < 16, rows, turned)
    high = jnp.where(me < 16, turned, rows)
    lane = lax.broadcasted_iota(I32, (128, 128), 1)
    line = lax.broadcasted_iota(I32, (128, 128), 0)
    for g in range(8):
        for half in range(2):
            a = 4 * g + 2 * half
            wanted = jnp.where(lane < SLOT, low[a : a + 1, :], high[a + 1 : a + 2, :]).astype(I32)
            match = ((line >> 5) == 2 * half + (lane >> 6)) & ((line & 31) == wanted)
            remap[g * 128 : (g + 1) * 128, half * 128 : (half + 1) * 128] = jnp.where(match, 1.0, 0.0).astype(BF16)
    for g in range(8):
        part = dot(remap[g * 128 : (g + 1) * 128, :], halo_cnt[g * 256 : (g + 1) * 256, :])
        bnd_cnt[g * 128 : (g + 1) * 128, :] = part.astype(BF16)
    remap_out = pltpu.make_async_copy(remap, remap_hbm, out_sem.at[2])
    remap_out.start()

    done(bnd, BND, 3, recv.at[4])
    done(bnd, BND, 9, recv.at[5])
    spread_sib(bnd, BND, 4, 12, b_sib_send, 11)
    for i in range(3):
        summed[third_of(i), :] += dot(bnd_cnt[0:512, third_of(i)], bnd[0:512, :], TN)

    done(column, COLUMN, 12, recv.at[8])
    spread_sib(column, COLUMN, 4, 12, h_sib_send, 9)

    done(bnd, BND, 4, recv.at[3])
    done(bnd, BND, 12, recv.at[11])
    bnd_out = pltpu.make_async_copy(bnd, bnd_hbm, out_sem.at[0])
    bnd_out.start()
    for i in range(3):
        summed[third_of(i), :] += dot(bnd_cnt[512:, third_of(i)], bnd[512:, :], TN)

    wn_in.wait()
    done(column, COLUMN, 16, recv.at[9])
    column_out = pltpu.make_async_copy(column, column_hbm, out_sem.at[1])
    column_out.start()
    for i in range(3):
        total = summed[third_of(i), :] + dot(column_cnt[:, third_of(i)], column[...], TN)
        mean = (total * jnp.concatenate([inverse[third_of(i), :]] * 8, axis=1)).astype(BF16)
        mixed = acc[third_of(i), :] + dot(mean, wn[...])
        out_buf[third_of(i), :] = jnp.maximum(mixed, 0.0).astype(BF16)
        pltpu.make_async_copy(out_buf.at[third_of(i), :], out_hbm.at[third_of(i), :], out_sem.at[3]).start()

    done(bnd, BND, 15, b_send)
    done(bnd, BND, 16, b_sib_send)
    done(pos, 16, 15, p_send)
    done(pos, 16, 16, p_sib_send)
    done(column, COLUMN, 15, h_send)
    done(column, COLUMN, 16, h_sib_send)
    part = tile_z.at[pl.ds(1, N_GRP - 1)]
    pltpu.make_async_copy(part, part, z_send).wait()
    bnd_out.wait()
    column_out.wait()
    remap_out.wait()
    pltpu.make_async_copy(out_buf, out_hbm, out_sem.at[3]).wait()


def finish_kernel(flag_hbm, fast_hbm, node_hbm, ws_hbm, wn_hbm, bnd_hbm, column_hbm, remap_hbm, hub_hbm, src_hbm, dst_hbm,
                  out_hbm,
                  flag, node, ws, wn, bnd, column, remap, hub_ids, edge_src, edge_dst, one_dst, one_src, col_of, summed, degree,
                  out_buf, sem):
    flag_in = pltpu.make_async_copy(flag_hbm, flag, sem.at[0])
    flag_in.start()
    parts = [pl.ds(i * 192, 192) for i in range(4)]
    ins = [pltpu.make_async_copy(fast_hbm.at[p, :], out_buf.at[p, :], sem.at[1 + i]) for i, p in enumerate(parts)]
    outs = [pltpu.make_async_copy(out_buf.at[p, :], out_hbm.at[p, :], sem.at[5 + i]) for i, p in enumerate(parts)]
    for one in ins:
        one.start()
    flag_in.wait()
    for one, two in zip(ins, outs):
        one.wait()
        two.start()
    for two in outs:
        two.wait()

    @pl.when(flag[0, 0] != 0)
    def _():
        grp = lax.axis_index("grp")
        me = lax.axis_index("dev")
        pairs = [(node_hbm, node), (ws_hbm, ws), (wn_hbm, wn), (bnd_hbm, bnd), (column_hbm, column), (remap_hbm, remap),
                 (hub_hbm, hub_ids), (src_hbm, edge_src), (dst_hbm, edge_dst)]
        copies = [pltpu.make_async_copy(a, b, sem.at[i]) for i, (a, b) in enumerate(pairs)]
        for one in copies:
            one.start()
        for one in copies:
            one.wait()
        owner, rank = hub_owner_rank(hub_ids[...])
        at_row = place(owner % N_DEV, me) * COLUMN + ((grp - owner // N_DEV) & 7) * 2 + rank
        choose = jnp.where(lax.broadcasted_iota(I32, (N_DEV * COLUMN, HUBS), 0) == at_row, 1.0, 0.0).astype(BF16)
        hubs = dot(choose, column[...], TN).astype(BF16)
        col_of[...] = edge_column(edge_src[...], me)
        degree[...] = jnp.zeros_like(degree)
        summed[...] = jnp.zeros_like(summed)

        @pl.loop(0, ROWS)
        def _(r):
            here = pl.ds(pl.multiple_of(r * 128, 128), 128)
            match = lax.broadcasted_iota(I32, (NPD, 128), 0) == edge_dst[pl.ds(r, 1), :]
            hit = jnp.where(match, 1.0, 0.0)
            one_dst[:, here] = hit.astype(BF16)
            degree[...] += jnp.sum(hit, axis=1, keepdims=True)

        def block(first, rows):
            n = rows.shape[0]

            @pl.loop(0, ROWS)
            def _(r):
                here = pl.ds(pl.multiple_of(r * 128, 128), 128)
                match = lax.broadcasted_iota(I32, (256, 128), 0) + first == col_of[pl.ds(r, 1), :]
                one_src[:, here] = jnp.where(match, 1.0, 0.0).astype(BF16)

            count = jnp.zeros((NPD, 256), F32)
            for i in range(STEPS):
                here = slice(i * STEP, (i + 1) * STEP)
                count = count + dot(one_dst[:, here], one_src[:, here], NT)
            upper = jnp.floor(count * (1.0 / 256.0)) * 256.0
            lower = count - upper
            summed[...] += dot(upper[:, 0:n].astype(BF16), rows) + dot(lower[:, 0:n].astype(BF16), rows)

        @pl.loop(0, 8)
        def _(g):
            lines = pl.ds(pl.multiple_of(g * 128, 128), 128)
            block(g * 256, dot(remap[lines, :], bnd[lines, :], TN).astype(BF16))

        @pl.loop(0, 3)
        def _(g):
            block(HALO + g * 256, node[pl.ds(pl.multiple_of(g * 256, 256), 256), :])

        block(HALO + NPD, hubs)
        mean = (summed[...] / degree[...]).astype(BF16)
        mixed = dot(node[...], ws[...]) + dot(mean, wn[...])
        out_buf[...] = jnp.maximum(mixed, 0.0).astype(BF16)
        last = pltpu.make_async_copy(out_buf, out_hbm, sem.at[0])
        last.start()
        last.wait()


def body(node_rows, w_self, w_neigh, hub_ids, bnd_idx, send_pos, edge_src, edge_dst):
    any_, vmem = pl.BlockSpec(memory_space=pl.ANY), pl.BlockSpec(memory_space=pltpu.VMEM)
    dma = pltpu.SemaphoreType.DMA
    src, dst = edge_src.reshape(ROWS, 128), edge_dst.reshape(ROWS, 128)
    scratch = [
        pltpu.VMEM((NPD, D), BF16),
        pltpu.VMEM((D, D), BF16),
        pltpu.VMEM((D, D), BF16),
        pltpu.VMEM((N_DEV * BND, D), BF16),
        pltpu.VMEM((N_DEV * 16, 128), BF16),
        pltpu.VMEM((N_DEV * COLUMN, D), BF16),
        pltpu.VMEM((N_GRP, 16, 128), BF16),
        pltpu.VMEM((N_DEV * BND, 256), BF16),
        pltpu.VMEM((ROWS, 128), I32),
        pltpu.VMEM((ROWS, 128), F32),
        pltpu.VMEM((NPD, STEP), BF16),
        pltpu.VMEM((LINES, STEP), BF16),
        pltpu.VMEM((LINES, NPD), F32),
        pltpu.VMEM((NPD, 128), F32),
        pltpu.VMEM((HALO_DIGITS * HALO_LINES, NPD), BF16),
        pltpu.VMEM((NPD, NPD), BF16),
        pltpu.VMEM((HUBS, NPD), BF16),
        pltpu.VMEM((N_DEV * COLUMN, NPD), BF16),
        pltpu.VMEM((N_DEV * BND, NPD), BF16),
        pltpu.VMEM((NPD, D), F32),
        pltpu.VMEM((NPD, D), F32),
        pltpu.VMEM((NPD, D), BF16),
        dma((3,)), dma((4,)), dma, dma, dma, dma, dma, dma, dma, dma((12,)),
    ]
    outs = [
        jax.ShapeDtypeStruct((NPD, D), BF16),
        jax.ShapeDtypeStruct((N_DEV * BND, D), BF16),
        jax.ShapeDtypeStruct((N_DEV * COLUMN, D), BF16),
        jax.ShapeDtypeStruct((N_DEV * BND, 256), BF16),
        jax.ShapeDtypeStruct((8, 128), I32),
    ]
    hub_row = hub_ids.reshape(1, HUBS)
    fast, bnd, column, remap, flag = pl.pallas_call(
        main_kernel,
        out_shape=outs,
        in_specs=[any_, any_, any_, vmem, vmem, vmem, vmem, vmem],
        out_specs=[any_, any_, any_, any_, vmem],
        scratch_shapes=scratch,
        compiler_params=pltpu.CompilerParams(
            collective_id=0, has_side_effects=True, vmem_limit_bytes=56 * 2**20
        ),
        name="sage_main",
    )(node_rows, w_self, w_neigh, hub_row, bnd_idx, send_pos, src, dst)
    scratch = [
        pltpu.SMEM((8, 128), I32),
        pltpu.VMEM((NPD, D), BF16),
        pltpu.VMEM((D, D), BF16),
        pltpu.VMEM((D, D), BF16),
        pltpu.VMEM((N_DEV * BND, D), BF16),
        pltpu.VMEM((N_DEV * COLUMN, D), BF16),
        pltpu.VMEM((N_DEV * BND, 256), BF16),
        pltpu.VMEM((1, HUBS), I32),
        pltpu.VMEM((ROWS, 128), I32),
        pltpu.VMEM((ROWS, 128), I32),
        pltpu.VMEM((NPD, E_DEV), BF16),
        pltpu.VMEM((256, E_DEV), BF16),
        pltpu.VMEM((ROWS, 128), I32),
        pltpu.VMEM((NPD, D), F32),
        pltpu.VMEM((NPD, 1), F32),
        pltpu.VMEM((NPD, D), BF16),
        dma((9,)),
    ]
    return pl.pallas_call(
        finish_kernel,
        out_shape=jax.ShapeDtypeStruct((NPD, D), BF16),
        in_specs=[any_] * 11,
        out_specs=any_,
        scratch_shapes=scratch,
        compiler_params=pltpu.CompilerParams(vmem_limit_bytes=56 * 2**20),
        name="sage_finish",
    )(flag, fast, node_rows, w_self, w_neigh, bnd, column, remap, hub_row, src, dst)


def solution(mesh):
    in_specs = (
        P(("grp", "dev"), None),
        P(),
        P(),
        P(),
        P(("grp", "dev"), None),
        P(("grp", "dev"), None, None),
        P(("grp", "dev")),
        P(("grp", "dev")),
    )
    out_specs = P(("grp", "dev"), None)
    return jax.shard_map(body, mesh=mesh, in_specs=in_specs, out_specs=out_specs, check_vma=False)
```

```python
import jax
import jax.numpy as jnp
from jax import lax
from jax.experimental import pallas as pl
from jax.experimental.pallas import tpu as pltpu
from jax.sharding import PartitionSpec as P

D = 1024
NPD = 768
HUBS = 64
BND = 32
SLOT = 64
E_DEV = 6144
ROWS = E_DEV // 128
N_DEV = 32
N_GRP = 8
HALO = N_DEV * SLOT
COLUMN = 2 * N_GRP
STEPS = 4
STEP_ROWS = ROWS // STEPS
STEP = STEP_ROWS * 128
HALO_DIGITS, HALO_BITS, HALO_LINES = 11, 2, 192
OWN_DIGITS, OWN_BITS, OWN_LINES, HUB_LINES = 8, 3, 96, 8
HUB_AT = HALO_LINES + OWN_LINES
DEGREE_AT = HUB_AT + HUB_LINES
LINES = DEGREE_AT + 8
LIMIT = 2.0**24
MESH = pl.DeviceIdType.MESH
NT = (((1,), (1,)), ((), ()))
TN = (((0,), (0,)), ((), ()))
BF16, F32, I32, I16 = jnp.bfloat16, jnp.float32, jnp.int32, jnp.int16


def dot(a, b, dims=(((1,), (0,)), ((), ()))):
    return lax.dot_general(a, b, dims, preferred_element_type=F32)


def place(dev, me):
    core = dev & 1
    dx = ((dev >> 3) - (me >> 3)) & 3
    dy = ((dev >> 1) - (me >> 1)) & 3
    du = jnp.where(core == 0, dx, dy)
    dv = jnp.where(core == 0, dy, dx)
    return 16 * (core ^ (me & 1)) + 4 * dv + du


def edge_column(src, me):
    slot = src - NPD
    is_halo = jnp.logical_and(slot >= 0, slot < HALO)
    halo = place((slot >> 6) & 31, me) * SLOT + (slot & 63)
    return jnp.where(is_halo, halo, jnp.where(src < NPD, src + HALO, src))


def hub_owner_rank(hub_ids):
    owner = hub_ids // NPD
    lines = lax.broadcasted_iota(I32, (N_DEV * N_GRP, HUBS), 0)
    member = jnp.where(lines == owner, 1.0, 0.0).astype(BF16)
    same = dot(member, member, TN)
    earlier = lax.broadcasted_iota(I32, (HUBS, HUBS), 0) < lax.broadcasted_iota(I32, (HUBS, HUBS), 1)
    rank = jnp.sum(jnp.where(earlier, same, 0.0), axis=0, keepdims=True)
    return owner, rank.astype(I32)


def main_kernel(node_hbm, ws_hbm, wn_hbm, hub_ids, bnd_idx, send_pos, edge_src, edge_dst,
                out_hbm, bnd_hbm, column_hbm, remap_hbm, flag,
                node, ws, wn, bnd, pos, column, tile_z, remap,
                line_of, weight_of, one_dst, one_src, packed, inverse,
                halo_cnt, own_cnt, hub_cnt, column_cnt, bnd_cnt, acc, summed, out_buf,
                in_sem, out_sem, b_send, b_sib_send, p_send, p_sib_send, h_send, h_sib_send, z_send, recv):
    grp = lax.axis_index("grp")
    me = lax.axis_index("dev")
    x, y, c = me // 8, (me // 2) % 4, me % 2
    sib = me + 1 - 2 * c

    def at(du, dv):
        dx, dy = du * (1 - c) + dv * c, dv * (1 - c) + du * c
        return (((x + dx) % 4) * 4 + (y + dy) % 4) * 2 + c

    node_in = pltpu.make_async_copy(node_hbm, node, in_sem.at[0])
    ws_in = pltpu.make_async_copy(ws_hbm, ws, in_sem.at[1])
    wn_in = pltpu.make_async_copy(wn_hbm, wn, in_sem.at[2])
    node_in.start()
    ws_in.start()
    wn_in.start()

    barrier = pltpu.get_barrier_semaphore()
    for near in [at(1, 0), at(3, 0), at(2, 0), at(0, 1), at(0, 3), at(0, 2), sib]:
        pl.semaphore_signal(barrier, inc=1, device_id=(grp, near), device_id_type=MESH)
    for o in range(1, N_GRP):
        pl.semaphore_signal(barrier, inc=1, device_id=((grp + o) % N_GRP, me), device_id_type=MESH)

    packed[...] = jnp.zeros_like(packed)

    def copy(src, dst, send, got, g, to):
        pltpu.make_async_remote_copy(src, dst, send, recv.at[got], device_id=(g, to), device_id_type=MESH).start()

    def blocks(ref, n, lo, count):
        return ref.at[pl.ds(lo * n, count * n), :]

    def spread_u(ref, n, send, got):
        for du in (1, 3, 2):
            copy(blocks(ref, n, 0, 1), blocks(ref, n, 4 - du, 1), send, got, grp, at(du, 0))

    def spread_v(ref, n, lo, count, send, got):
        for dv in (1, 3, 2):
            copy(blocks(ref, n, lo, count), blocks(ref, n, 4 * (4 - dv) + lo, count), send, got, grp, at(0, dv))

    def spread_sib(ref, n, lo, count, send, got):
        copy(blocks(ref, n, lo, count), blocks(ref, n, 16 + lo, count), send, got, grp, sib)

    def done(ref, n, count, sem):
        part = blocks(ref, n, 0, count)
        pltpu.make_async_copy(part, part, sem).wait()

    owner, rank = hub_owner_rank(hub_ids[...])
    local = hub_ids[...] - (grp * N_DEV + me) * NPD
    wanted = jnp.concatenate([local, bnd_idx[...]], axis=1)
    pick = jnp.where(lax.broadcasted_iota(I32, (NPD, HUBS + BND), 0) == wanted, 1.0, 0.0).astype(BF16)
    by_rank = jnp.where(lax.broadcasted_iota(I32, (8, HUBS), 0) == rank, 1.0, 0.0).astype(BF16)
    positions = send_pos[0].astype(F32)
    pos[0:16, 0:SLOT] = positions[0:16].astype(BF16)
    pos[0:16, SLOT:128] = positions[16:32].astype(BF16)
    node_in.wait()
    rows = dot(pick, node[...], TN).astype(BF16)
    bnd[0:BND, :] = rows[HUBS:]
    pair = dot(by_rank, rows[0:HUBS])
    tile = jnp.concatenate([pair[0:2, q * 128 : (q + 1) * 128] for q in range(8)], axis=0)
    tile_z[0] = tile.astype(BF16)

    pl.semaphore_wait(barrier, 7 + N_GRP - 1)
    for o in range(1, N_GRP):
        copy(tile_z.at[0], tile_z.at[o], z_send, 2, (grp + o) % N_GRP, me)
    spread_u(pos, 16, p_send, 1)
    spread_u(bnd, BND, b_send, 0)
    spread_sib(bnd, BND, 0, 1, b_sib_send, 3)

    col = edge_column(edge_src[...], me)
    third = lambda n: (n * 43) >> 7
    own = col - HALO
    hub = own - NPD
    halo_digit, own_digit = third(col >> 6), third(own >> 5)
    line = jnp.where(own < 0, col - HALO_LINES * halo_digit,
                     jnp.where(hub < 0, HALO_LINES + own - OWN_LINES * own_digit, HUB_AT + (hub & 7)))
    shift = jnp.where(own < 0, HALO_BITS * halo_digit, OWN_BITS * jnp.where(hub < 0, own_digit, hub >> 3))
    line_of[...] = line
    weight_of[...] = jnp.left_shift(jnp.ones_like(shift), shift).astype(F32)

    @pl.loop(0, STEPS)
    def _(step):
        zero, one = jnp.zeros((), BF16), jnp.ones((), BF16)
        for r in range(STEP_ROWS):
            row = pl.ds(step * STEP_ROWS + r, 1)
            here = slice(r * 128, (r + 1) * 128)
            d = edge_dst[row, :].astype(I16)
            s = line_of[row, :].astype(I16)
            w = weight_of[row, :].astype(BF16)
            one_dst[:, here] = jnp.where(lax.broadcasted_iota(I16, (NPD, 128), 0) == d, one, zero)
            lines = lax.broadcasted_iota(I16, (LINES, 128), 0)
            value = jnp.where(lines == s, jnp.broadcast_to(w, (LINES, 128)), zero)
            one_src[:, here] = jnp.where(lines >= DEGREE_AT, one, value)
        packed[...] += dot(one_src[...], one_dst[...], NT)

        @pl.when(step == 0)
        def _():
            spread_v(bnd, BND, 0, 1, b_send, 4)

        @pl.when(step == 3)
        def _():
            done(pos, 16, 3, recv.at[1])
            spread_v(pos, 16, 0, 4, p_send, 6)
            done(bnd, BND, 3, recv.at[0])
            spread_v(bnd, BND, 1, 3, b_send, 5)
            spread_sib(bnd, BND, 1, 3, b_sib_send, 3)

            part = tile_z.at[pl.ds(1, N_GRP - 1)]
            pltpu.make_async_copy(part, part, recv.at[2]).wait()
            tiles = [tile_z[o].astype(F32) for o in range(N_GRP)]
            for q in range(8):
                rows = jnp.concatenate([t[2 * q : 2 * q + 2, :] for t in tiles], axis=0)
                column[0:COLUMN, q * 128 : (q + 1) * 128] = rows.astype(BF16)
            spread_u(column, COLUMN, h_send, 7)

    bnd_out = pltpu.make_async_copy(bnd, bnd_hbm, out_sem.at[0])
    column_out = pltpu.make_async_copy(column, column_hbm, out_sem.at[1])
    remap_out = pltpu.make_async_copy(remap, remap_hbm, out_sem.at[2])

    def third_of(i):
        return slice(i * 256, (i + 1) * 256)

    def task(run):
        pl.when(me >= 0)(run)

    @task
    def _():
        total = jnp.zeros((1, NPD), I32)
        ints = packed[0:HALO_LINES, :].astype(I32)
        for i in range(HALO_DIGITS):
            digit = ints >> (HALO_BITS * i)
            if i < HALO_DIGITS - 1:
                digit = digit & (2**HALO_BITS - 1)
            total = total + jnp.sum(digit, axis=0, keepdims=True)
            halo_cnt[i * HALO_LINES : (i + 1) * HALO_LINES, :] = digit.astype(F32).astype(BF16)
        ints = packed[HALO_LINES:DEGREE_AT, :].astype(I32)
        hub_parts = []
        for i in range(OWN_DIGITS):
            digit = ints >> (OWN_BITS * i)
            if i < OWN_DIGITS - 1:
                digit = digit & (2**OWN_BITS - 1)
            total = total + jnp.sum(digit, axis=0, keepdims=True)
            digit = digit.astype(F32)
            own_cnt[i * OWN_LINES : (i + 1) * OWN_LINES, :] = digit[0:OWN_LINES].astype(BF16)
            hub_parts.append(digit[OWN_LINES:])
        hub_cnt[...] = jnp.concatenate(hub_parts, axis=0).astype(BF16)

        degree = packed[DEGREE_AT : DEGREE_AT + 1, :]
        largest = jnp.max(packed[0:DEGREE_AT, :], axis=0, keepdims=True)
        bad = (total != degree.astype(I32)) | (largest >= LIMIT) | (degree > 256.0)
        flag[...] = jnp.broadcast_to(jnp.max(jnp.where(bad, 1, 0), axis=1, keepdims=True), (8, 128))
        inverse[...] = jnp.transpose(jnp.broadcast_to(1.0 / degree, (128, NPD)))

    @task
    def _():
        ws_in.wait()
        for i in range(3):
            acc[third_of(i), :] = dot(node[third_of(i), :], ws[...])

    @task
    def _():
        done(column, COLUMN, 3, recv.at[7])
        spread_v(column, COLUMN, 0, 4, h_send, 8)
        spread_sib(column, COLUMN, 0, 4, h_sib_send, 9)

    @task
    def _():
        for i in range(3):
            summed[third_of(i), :] = dot(own_cnt[0:NPD, third_of(i)], node[...], TN)

    @task
    def _():
        at_row = place(owner % N_DEV, me) * COLUMN + ((grp - owner // N_DEV) & 7) * 2 + rank
        choose = jnp.where(lax.broadcasted_iota(I32, (N_DEV * COLUMN, HUBS), 0) == at_row, 1.0, 0.0).astype(BF16)
        column_cnt[...] = dot(choose, hub_cnt[...]).astype(BF16)

    @task
    def _():
        done(pos, 16, 12, recv.at[6])
        spread_sib(pos, 16, 0, 16, p_sib_send, 10)

    @task
    def _():
        done(pos, 16, 16, recv.at[10])
        every = pos[...].astype(F32).reshape(N_DEV, 16, 128)
        mine = lax.broadcasted_iota(I32, (N_DEV, 16, 128), 1) == me % 16
        rows = jnp.sum(jnp.where(mine, every, 0.0), axis=1)
        turned = pltpu.roll(rows, SLOT, 1)
        low = jnp.where(me < 16, rows, turned)
        high = jnp.where(me < 16, turned, rows)
        lane = lax.broadcasted_iota(I32, (128, 128), 1)
        line = lax.broadcasted_iota(I32, (128, 128), 0)
        for g in range(8):
            for half in range(2):
                a = 4 * g + 2 * half
                wanted = jnp.where(lane < SLOT, low[a : a + 1, :], high[a + 1 : a + 2, :]).astype(I32)
                match = ((line >> 5) == 2 * half + (lane >> 6)) & ((line & 31) == wanted)
                remap[g * 128 : (g + 1) * 128, half * 128 : (half + 1) * 128] = jnp.where(match, 1.0, 0.0).astype(BF16)
        for g in range(8):
            part = dot(remap[g * 128 : (g + 1) * 128, :], halo_cnt[g * 256 : (g + 1) * 256, :])
            bnd_cnt[g * 128 : (g + 1) * 128, :] = part.astype(BF16)
        remap_out.start()

    @task
    def _():
        done(bnd, BND, 3, recv.at[4])
        done(bnd, BND, 9, recv.at[5])
        spread_sib(bnd, BND, 4, 12, b_sib_send, 11)

    @task
    def _():
        for i in range(3):
            summed[third_of(i), :] += dot(bnd_cnt[0:512, third_of(i)], bnd[0:512, :], TN)

    @task
    def _():
        done(column, COLUMN, 12, recv.at[8])
        spread_sib(column, COLUMN, 4, 12, h_sib_send, 9)

    @task
    def _():
        done(bnd, BND, 4, recv.at[3])
        done(bnd, BND, 12, recv.at[11])
        bnd_out.start()
        for i in range(3):
            summed[third_of(i), :] += dot(bnd_cnt[512:, third_of(i)], bnd[512:, :], TN)

    @task
    def _():
        wn_in.wait()
        done(column, COLUMN, 16, recv.at[9])
        column_out.start()
        for i in range(3):
            total = summed[third_of(i), :] + dot(column_cnt[:, third_of(i)], column[...], TN)
            mean = (total * jnp.concatenate([inverse[third_of(i), :]] * 8, axis=1)).astype(BF16)
            mixed = acc[third_of(i), :] + dot(mean, wn[...])
            out_buf[third_of(i), :] = jnp.maximum(mixed, 0.0).astype(BF16)
            pltpu.make_async_copy(out_buf.at[third_of(i), :], out_hbm.at[third_of(i), :], out_sem.at[3]).start()

    done(bnd, BND, 15, b_send)
    done(bnd, BND, 16, b_sib_send)
    done(pos, 16, 15, p_send)
    done(pos, 16, 16, p_sib_send)
    done(column, COLUMN, 15, h_send)
    done(column, COLUMN, 16, h_sib_send)
    part = tile_z.at[pl.ds(1, N_GRP - 1)]
    pltpu.make_async_copy(part, part, z_send).wait()
    bnd_out.wait()
    column_out.wait()
    remap_out.wait()
    pltpu.make_async_copy(out_buf, out_hbm, out_sem.at[3]).wait()


def finish_kernel(flag_hbm, fast_hbm, node_hbm, ws_hbm, wn_hbm, bnd_hbm, column_hbm, remap_hbm, hub_hbm, src_hbm, dst_hbm,
                  out_hbm,
                  flag, node, ws, wn, bnd, column, remap, hub_ids, edge_src, edge_dst, one_dst, one_src, col_of, summed, degree,
                  out_buf, sem):
    flag_in = pltpu.make_async_copy(flag_hbm, flag, sem.at[0])
    flag_in.start()
    parts = [pl.ds(i * 192, 192) for i in range(4)]
    ins = [pltpu.make_async_copy(fast_hbm.at[p, :], out_buf.at[p, :], sem.at[1 + i]) for i, p in enumerate(parts)]
    outs = [pltpu.make_async_copy(out_buf.at[p, :], out_hbm.at[p, :], sem.at[5 + i]) for i, p in enumerate(parts)]
    for one in ins:
        one.start()
    flag_in.wait()
    for one, two in zip(ins, outs):
        one.wait()
        two.start()
    for two in outs:
        two.wait()

    @pl.when(flag[0, 0] != 0)
    def _():
        grp = lax.axis_index("grp")
        me = lax.axis_index("dev")
        pairs = [(node_hbm, node), (ws_hbm, ws), (wn_hbm, wn), (bnd_hbm, bnd), (column_hbm, column), (remap_hbm, remap),
                 (hub_hbm, hub_ids), (src_hbm, edge_src), (dst_hbm, edge_dst)]
        copies = [pltpu.make_async_copy(a, b, sem.at[i]) for i, (a, b) in enumerate(pairs)]
        for one in copies:
            one.start()
        for one in copies:
            one.wait()
        owner, rank = hub_owner_rank(hub_ids[...])
        at_row = place(owner % N_DEV, me) * COLUMN + ((grp - owner // N_DEV) & 7) * 2 + rank
        choose = jnp.where(lax.broadcasted_iota(I32, (N_DEV * COLUMN, HUBS), 0) == at_row, 1.0, 0.0).astype(BF16)
        hubs = dot(choose, column[...], TN).astype(BF16)
        col_of[...] = edge_column(edge_src[...], me)
        degree[...] = jnp.zeros_like(degree)
        summed[...] = jnp.zeros_like(summed)

        @pl.loop(0, ROWS)
        def _(r):
            here = pl.ds(pl.multiple_of(r * 128, 128), 128)
            match = lax.broadcasted_iota(I32, (NPD, 128), 0) == edge_dst[pl.ds(r, 1), :]
            hit = jnp.where(match, 1.0, 0.0)
            one_dst[:, here] = hit.astype(BF16)
            degree[...] += jnp.sum(hit, axis=1, keepdims=True)

        def block(first, rows):
            n = rows.shape[0]

            @pl.loop(0, ROWS)
            def _(r):
                here = pl.ds(pl.multiple_of(r * 128, 128), 128)
                match = lax.broadcasted_iota(I32, (256, 128), 0) + first == col_of[pl.ds(r, 1), :]
                one_src[:, here] = jnp.where(match, 1.0, 0.0).astype(BF16)

            count = jnp.zeros((NPD, 256), F32)
            for i in range(STEPS):
                here = slice(i * STEP, (i + 1) * STEP)
                count = count + dot(one_dst[:, here], one_src[:, here], NT)
            upper = jnp.floor(count * (1.0 / 256.0)) * 256.0
            lower = count - upper
            summed[...] += dot(upper[:, 0:n].astype(BF16), rows) + dot(lower[:, 0:n].astype(BF16), rows)

        @pl.loop(0, 8)
        def _(g):
            lines = pl.ds(pl.multiple_of(g * 128, 128), 128)
            block(g * 256, dot(remap[lines, :], bnd[lines, :], TN).astype(BF16))

        @pl.loop(0, 3)
        def _(g):
            block(HALO + g * 256, node[pl.ds(pl.multiple_of(g * 256, 256), 256), :])

        block(HALO + NPD, hubs)
        mean = (summed[...] / degree[...]).astype(BF16)
        mixed = dot(node[...], ws[...]) + dot(mean, wn[...])
        out_buf[...] = jnp.maximum(mixed, 0.0).astype(BF16)
        last = pltpu.make_async_copy(out_buf, out_hbm, sem.at[0])
        last.start()
        last.wait()


def body(node_rows, w_self, w_neigh, hub_ids, bnd_idx, send_pos, edge_src, edge_dst):
    any_, vmem = pl.BlockSpec(memory_space=pl.ANY), pl.BlockSpec(memory_space=pltpu.VMEM)
    dma = pltpu.SemaphoreType.DMA
    src, dst = edge_src.reshape(ROWS, 128), edge_dst.reshape(ROWS, 128)
    scratch = [
        pltpu.VMEM((NPD, D), BF16),
        pltpu.VMEM((D, D), BF16),
        pltpu.VMEM((D, D), BF16),
        pltpu.VMEM((N_DEV * BND, D), BF16),
        pltpu.VMEM((N_DEV * 16, 128), BF16),
        pltpu.VMEM((N_DEV * COLUMN, D), BF16),
        pltpu.VMEM((N_GRP, 16, 128), BF16),
        pltpu.VMEM((N_DEV * BND, 256), BF16),
        pltpu.VMEM((ROWS, 128), I32),
        pltpu.VMEM((ROWS, 128), F32),
        pltpu.VMEM((NPD, STEP), BF16),
        pltpu.VMEM((LINES, STEP), BF16),
        pltpu.VMEM((LINES, NPD), F32),
        pltpu.VMEM((NPD, 128), F32),
        pltpu.VMEM((HALO_DIGITS * HALO_LINES, NPD), BF16),
        pltpu.VMEM((NPD, NPD), BF16),
        pltpu.VMEM((HUBS, NPD), BF16),
        pltpu.VMEM((N_DEV * COLUMN, NPD), BF16),
        pltpu.VMEM((N_DEV * BND, NPD), BF16),
        pltpu.VMEM((NPD, D), F32),
        pltpu.VMEM((NPD, D), F32),
        pltpu.VMEM((NPD, D), BF16),
        dma((3,)), dma((4,)), dma, dma, dma, dma, dma, dma, dma, dma((12,)),
    ]
    outs = [
        jax.ShapeDtypeStruct((NPD, D), BF16),
        jax.ShapeDtypeStruct((N_DEV * BND, D), BF16),
        jax.ShapeDtypeStruct((N_DEV * COLUMN, D), BF16),
        jax.ShapeDtypeStruct((N_DEV * BND, 256), BF16),
        jax.ShapeDtypeStruct((8, 128), I32),
    ]
    hub_row = hub_ids.reshape(1, HUBS)
    fast, bnd, column, remap, flag = pl.pallas_call(
        main_kernel,
        out_shape=outs,
        in_specs=[any_, any_, any_, vmem, vmem, vmem, vmem, vmem],
        out_specs=[any_, any_, any_, any_, vmem],
        scratch_shapes=scratch,
        compiler_params=pltpu.CompilerParams(
            collective_id=0, has_side_effects=True, vmem_limit_bytes=56 * 2**20
        ),
        name="sage_main",
    )(node_rows, w_self, w_neigh, hub_row, bnd_idx, send_pos, src, dst)
    scratch = [
        pltpu.SMEM((8, 128), I32),
        pltpu.VMEM((NPD, D), BF16),
        pltpu.VMEM((D, D), BF16),
        pltpu.VMEM((D, D), BF16),
        pltpu.VMEM((N_DEV * BND, D), BF16),
        pltpu.VMEM((N_DEV * COLUMN, D), BF16),
        pltpu.VMEM((N_DEV * BND, 256), BF16),
        pltpu.VMEM((1, HUBS), I32),
        pltpu.VMEM((ROWS, 128), I32),
        pltpu.VMEM((ROWS, 128), I32),
        pltpu.VMEM((NPD, E_DEV), BF16),
        pltpu.VMEM((256, E_DEV), BF16),
        pltpu.VMEM((ROWS, 128), I32),
        pltpu.VMEM((NPD, D), F32),
        pltpu.VMEM((NPD, 1), F32),
        pltpu.VMEM((NPD, D), BF16),
        dma((9,)),
    ]
    return pl.pallas_call(
        finish_kernel,
        out_shape=jax.ShapeDtypeStruct((NPD, D), BF16),
        in_specs=[any_] * 11,
        out_specs=any_,
        scratch_shapes=scratch,
        compiler_params=pltpu.CompilerParams(vmem_limit_bytes=56 * 2**20),
        name="sage_finish",
    )(flag, fast, node_rows, w_self, w_neigh, bnd, column, remap, hub_row, src, dst)


def solution(mesh):
    in_specs = (
        P(("grp", "dev"), None),
        P(),
        P(),
        P(),
        P(("grp", "dev"), None),
        P(("grp", "dev"), None, None),
        P(("grp", "dev")),
        P(("grp", "dev")),
    )
    out_specs = P(("grp", "dev"), None)
    return jax.shard_map(body, mesh=mesh, in_specs=in_specs, out_specs=out_specs, check_vma=False)
```

```python
import jax
import jax.numpy as jnp
from jax import lax
from jax.experimental import pallas as pl
from jax.experimental.pallas import tpu as pltpu
from jax.sharding import PartitionSpec as P

D = 1024
NPD = 768
HUBS = 64
BND = 32
SLOT = 64
E_DEV = 6144
ROWS = E_DEV // 128
N_DEV = 32
N_GRP = 8
HALO = N_DEV * SLOT
COLUMN = 2 * N_GRP
STEPS = 4
STEP_ROWS = ROWS // STEPS
STEP = STEP_ROWS * 128
HALO_DIGITS, HALO_BITS, HALO_LINES = 11, 2, 192
OWN_DIGITS, OWN_BITS, OWN_LINES, HUB_LINES = 8, 3, 96, 8
HUB_AT = HALO_LINES + OWN_LINES
DEGREE_AT = HUB_AT + HUB_LINES
LINES = DEGREE_AT + 8
LIMIT = 2.0**24
MESH = pl.DeviceIdType.MESH
NT = (((1,), (1,)), ((), ()))
TN = (((0,), (0,)), ((), ()))
BF16, F32, I32, I16 = jnp.bfloat16, jnp.float32, jnp.int32, jnp.int16


def dot(a, b, dims=(((1,), (0,)), ((), ()))):
    return lax.dot_general(a, b, dims, preferred_element_type=F32)


def place(dev, me):
    core = dev & 1
    dx = ((dev >> 3) - (me >> 3)) & 3
    dy = ((dev >> 1) - (me >> 1)) & 3
    du = jnp.where(core == 0, dx, dy)
    dv = jnp.where(core == 0, dy, dx)
    return 16 * (core ^ (me & 1)) + 4 * dv + du


def edge_column(src, me):
    slot = src - NPD
    is_halo = jnp.logical_and(slot >= 0, slot < HALO)
    halo = place((slot >> 6) & 31, me) * SLOT + (slot & 63)
    return jnp.where(is_halo, halo, jnp.where(src < NPD, src + HALO, src))


def hub_owner_rank(hub_ids):
    owner = hub_ids // NPD
    lines = lax.broadcasted_iota(I32, (N_DEV * N_GRP, HUBS), 0)
    member = jnp.where(lines == owner, 1.0, 0.0).astype(BF16)
    same = dot(member, member, TN)
    earlier = lax.broadcasted_iota(I32, (HUBS, HUBS), 0) < lax.broadcasted_iota(I32, (HUBS, HUBS), 1)
    rank = jnp.sum(jnp.where(earlier, same, 0.0), axis=0, keepdims=True)
    return owner, rank.astype(I32)


def main_kernel(node_hbm, ws_hbm, wn_hbm, hub_ids, bnd_idx, send_pos, edge_src, edge_dst,
                out_hbm, bnd_hbm, column_hbm, remap_hbm, flag,
                node, ws, wn, bnd, pos, column, tile_z, remap,
                line_of, weight_of, one_dst, one_src, packed, inverse,
                halo_cnt, own_cnt, hub_cnt, column_cnt, bnd_cnt, acc, summed, out_buf,
                in_sem, out_sem, b_send, b_sib_send, p_send, p_sib_send, h_send, h_sib_send, z_send, recv):
    grp = lax.axis_index("grp")
    me = lax.axis_index("dev")
    x, y, c = me // 8, (me // 2) % 4, me % 2
    sib = me + 1 - 2 * c

    def at(du, dv):
        dx, dy = du * (1 - c) + dv * c, dv * (1 - c) + du * c
        return (((x + dx) % 4) * 4 + (y + dy) % 4) * 2 + c

    node_in = pltpu.make_async_copy(node_hbm, node, in_sem.at[0])
    ws_in = pltpu.make_async_copy(ws_hbm, ws, in_sem.at[1])
    wn_in = pltpu.make_async_copy(wn_hbm, wn, in_sem.at[2])
    node_in.start()
    ws_in.start()
    wn_in.start()

    barrier = pltpu.get_barrier_semaphore()
    for o in (4, 5, 3, 6, 2, 7, 1):
        pl.semaphore_signal(barrier, inc=1, device_id=((grp + o) % N_GRP, me), device_id_type=MESH)
    for near in [at(1, 0), at(3, 0), at(2, 0), at(0, 1), at(0, 3), at(0, 2), sib]:
        pl.semaphore_signal(barrier, inc=1, device_id=(grp, near), device_id_type=MESH)

    packed[...] = jnp.zeros_like(packed)

    def copy(src, dst, send, got, g, to):
        pltpu.make_async_remote_copy(src, dst, send, recv.at[got], device_id=(g, to), device_id_type=MESH).start()

    def blocks(ref, n, lo, count):
        return ref.at[pl.ds(lo * n, count * n), :]

    def spread_u(ref, n, send, got):
        for du in (1, 3, 2):
            copy(blocks(ref, n, 0, 1), blocks(ref, n, 4 - du, 1), send, got, grp, at(du, 0))

    def spread_v(ref, n, lo, count, send, got):
        for dv in (1, 3, 2):
            copy(blocks(ref, n, lo, count), blocks(ref, n, 4 * (4 - dv) + lo, count), send, got, grp, at(0, dv))

    def spread_sib(ref, n, lo, count, send, got):
        copy(blocks(ref, n, lo, count), blocks(ref, n, 16 + lo, count), send, got, grp, sib)

    def done(ref, n, count, sem):
        part = blocks(ref, n, 0, count)
        pltpu.make_async_copy(part, part, sem).wait()

    owner, rank = hub_owner_rank(hub_ids[...])
    local = hub_ids[...] - (grp * N_DEV + me) * NPD
    wanted = jnp.concatenate([local, bnd_idx[...]], axis=1)
    pick = jnp.where(lax.broadcasted_iota(I32, (NPD, HUBS + BND), 0) == wanted, 1.0, 0.0).astype(BF16)
    by_rank = jnp.where(lax.broadcasted_iota(I32, (8, HUBS), 0) == rank, 1.0, 0.0).astype(BF16)
    positions = send_pos[0].astype(F32)
    pos[0:16, 0:SLOT] = positions[0:16].astype(BF16)
    pos[0:16, SLOT:128] = positions[16:32].astype(BF16)
    node_in.wait()
    rows = dot(pick, node[...], TN).astype(BF16)
    bnd[0:BND, :] = rows[HUBS:]
    pair = dot(by_rank, rows[0:HUBS])
    tile = jnp.concatenate([pair[0:2, q * 128 : (q + 1) * 128] for q in range(8)], axis=0)
    tile_z[0] = tile.astype(BF16)

    pl.semaphore_wait(barrier, 7 + N_GRP - 1)
    for o in (4, 5, 3, 6, 2, 7, 1):
        copy(tile_z.at[0], tile_z.at[o], z_send, 2, (grp + o) % N_GRP, me)
    spread_u(pos, 16, p_send, 1)
    spread_u(bnd, BND, b_send, 0)
    spread_sib(bnd, BND, 0, 1, b_sib_send, 3)

    col = edge_column(edge_src[...], me)
    third = lambda n: (n * 43) >> 7
    own = col - HALO
    hub = own - NPD
    halo_digit, own_digit = third(col >> 6), third(own >> 5)
    line = jnp.where(own < 0, col - HALO_LINES * halo_digit,
                     jnp.where(hub < 0, HALO_LINES + own - OWN_LINES * own_digit, HUB_AT + (hub & 7)))
    shift = jnp.where(own < 0, HALO_BITS * halo_digit, OWN_BITS * jnp.where(hub < 0, own_digit, hub >> 3))
    line_of[...] = line
    weight_of[...] = jnp.left_shift(jnp.ones_like(shift), shift).astype(F32)

    @pl.loop(0, STEPS)
    def _(step):
        zero, one = jnp.zeros((), BF16), jnp.ones((), BF16)
        for r in range(STEP_ROWS):
            row = pl.ds(step * STEP_ROWS + r, 1)
            here = slice(r * 128, (r + 1) * 128)
            d = edge_dst[row, :].astype(I16)
            s = line_of[row, :].astype(I16)
            w = weight_of[row, :].astype(BF16)
            one_dst[:, here] = jnp.where(lax.broadcasted_iota(I16, (NPD, 128), 0) == d, one, zero)
            lines = lax.broadcasted_iota(I16, (LINES, 128), 0)
            value = jnp.where(lines == s, jnp.broadcast_to(w, (LINES, 128)), zero)
            one_src[:, here] = jnp.where(lines >= DEGREE_AT, one, value)
        packed[...] += dot(one_src[...], one_dst[...], NT)

        @pl.when(step == 0)
        def _():
            spread_v(bnd, BND, 0, 1, b_send, 4)

        @pl.when(step == 3)
        def _():
            part = tile_z.at[pl.ds(1, N_GRP - 1)]
            pltpu.make_async_copy(part, part, recv.at[2]).wait()
            tiles = [tile_z[o].astype(F32) for o in range(N_GRP)]
            for q in range(8):
                rows = jnp.concatenate([t[2 * q : 2 * q + 2, :] for t in tiles], axis=0)
                column[0:COLUMN, q * 128 : (q + 1) * 128] = rows.astype(BF16)
            spread_u(column, COLUMN, h_send, 7)

            done(pos, 16, 3, recv.at[1])
            spread_v(pos, 16, 0, 4, p_send, 6)
            done(bnd, BND, 3, recv.at[0])
            spread_v(bnd, BND, 1, 3, b_send, 5)
            spread_sib(bnd, BND, 1, 3, b_sib_send, 3)

    bnd_out = pltpu.make_async_copy(bnd, bnd_hbm, out_sem.at[0])
    column_out = pltpu.make_async_copy(column, column_hbm, out_sem.at[1])
    remap_out = pltpu.make_async_copy(remap, remap_hbm, out_sem.at[2])

    def third_of(i):
        return slice(i * 256, (i + 1) * 256)

    def task(run):
        pl.when(me >= 0)(run)

    @task
    def _():
        total = jnp.zeros((1, NPD), I32)
        ints = packed[0:HALO_LINES, :].astype(I32)
        for i in range(HALO_DIGITS):
            digit = ints >> (HALO_BITS * i)
            if i < HALO_DIGITS - 1:
                digit = digit & (2**HALO_BITS - 1)
            total = total + jnp.sum(digit, axis=0, keepdims=True)
            halo_cnt[i * HALO_LINES : (i + 1) * HALO_LINES, :] = digit.astype(F32).astype(BF16)
        ints = packed[HALO_LINES:DEGREE_AT, :].astype(I32)
        hub_parts = []
        for i in range(OWN_DIGITS):
            digit = ints >> (OWN_BITS * i)
            if i < OWN_DIGITS - 1:
                digit = digit & (2**OWN_BITS - 1)
            total = total + jnp.sum(digit, axis=0, keepdims=True)
            digit = digit.astype(F32)
            own_cnt[i * OWN_LINES : (i + 1) * OWN_LINES, :] = digit[0:OWN_LINES].astype(BF16)
            hub_parts.append(digit[OWN_LINES:])
        hub_cnt[...] = jnp.concatenate(hub_parts, axis=0).astype(BF16)

        degree = packed[DEGREE_AT : DEGREE_AT + 1, :]
        largest = jnp.max(packed[0:DEGREE_AT, :], axis=0, keepdims=True)
        bad = (total != degree.astype(I32)) | (largest >= LIMIT) | (degree > 256.0)
        flag[...] = jnp.broadcast_to(jnp.max(jnp.where(bad, 1, 0), axis=1, keepdims=True), (8, 128))
        inverse[...] = jnp.transpose(jnp.broadcast_to(1.0 / degree, (128, NPD)))

    @task
    def _():
        ws_in.wait()
        for i in range(3):
            acc[third_of(i), :] = dot(node[third_of(i), :], ws[...])

    @task
    def _():
        done(column, COLUMN, 3, recv.at[7])
        spread_v(column, COLUMN, 0, 4, h_send, 8)
        spread_sib(column, COLUMN, 0, 4, h_sib_send, 9)

    @task
    def _():
        for i in range(3):
            summed[third_of(i), :] = dot(own_cnt[0:NPD, third_of(i)], node[...], TN)

    @task
    def _():
        at_row = place(owner % N_DEV, me) * COLUMN + ((grp - owner // N_DEV) & 7) * 2 + rank
        choose = jnp.where(lax.broadcasted_iota(I32, (N_DEV * COLUMN, HUBS), 0) == at_row, 1.0, 0.0).astype(BF16)
        column_cnt[...] = dot(choose, hub_cnt[...]).astype(BF16)

    @task
    def _():
        done(pos, 16, 12, recv.at[6])
        spread_sib(pos, 16, 0, 16, p_sib_send, 10)

    @task
    def _():
        done(pos, 16, 16, recv.at[10])
        every = pos[...].astype(F32).reshape(N_DEV, 16, 128)
        mine = lax.broadcasted_iota(I32, (N_DEV, 16, 128), 1) == me % 16
        rows = jnp.sum(jnp.where(mine, every, 0.0), axis=1)
        turned = pltpu.roll(rows, SLOT, 1)
        low = jnp.where(me < 16, rows, turned)
        high = jnp.where(me < 16, turned, rows)
        lane = lax.broadcasted_iota(I32, (128, 128), 1)
        line = lax.broadcasted_iota(I32, (128, 128), 0)
        for g in range(8):
            for half in range(2):
                a = 4 * g + 2 * half
                wanted = jnp.where(lane < SLOT, low[a : a + 1, :], high[a + 1 : a + 2, :]).astype(I32)
                match = ((line >> 5) == 2 * half + (lane >> 6)) & ((line & 31) == wanted)
                remap[g * 128 : (g + 1) * 128, half * 128 : (half + 1) * 128] = jnp.where(match, 1.0, 0.0).astype(BF16)
        for g in range(8):
            part = dot(remap[g * 128 : (g + 1) * 128, :], halo_cnt[g * 256 : (g + 1) * 256, :])
            bnd_cnt[g * 128 : (g + 1) * 128, :] = part.astype(BF16)
        remap_out.start()

    @task
    def _():
        done(bnd, BND, 3, recv.at[4])
        done(bnd, BND, 9, recv.at[5])
        spread_sib(bnd, BND, 4, 12, b_sib_send, 11)

    @task
    def _():
        for i in range(3):
            summed[third_of(i), :] += dot(bnd_cnt[0:512, third_of(i)], bnd[0:512, :], TN)

    @task
    def _():
        done(column, COLUMN, 12, recv.at[8])
        spread_sib(column, COLUMN, 4, 12, h_sib_send, 9)
        for i in range(3):
            summed[third_of(i), :] += dot(column_cnt[0:256, third_of(i)], column[0:256, :], TN)

    @task
    def _():
        done(bnd, BND, 4, recv.at[3])
        done(bnd, BND, 12, recv.at[11])
        bnd_out.start()
        for i in range(3):
            summed[third_of(i), :] += dot(bnd_cnt[512:, third_of(i)], bnd[512:, :], TN)

    @task
    def _():
        wn_in.wait()
        done(column, COLUMN, 16, recv.at[9])
        column_out.start()
        for i in range(3):
            total = summed[third_of(i), :] + dot(column_cnt[256:, third_of(i)], column[256:, :], TN)
            mean = (total * jnp.concatenate([inverse[third_of(i), :]] * 8, axis=1)).astype(BF16)
            mixed = acc[third_of(i), :] + dot(mean, wn[...])
            out_buf[third_of(i), :] = jnp.maximum(mixed, 0.0).astype(BF16)
            pltpu.make_async_copy(out_buf.at[third_of(i), :], out_hbm.at[third_of(i), :], out_sem.at[3]).start()

    done(bnd, BND, 15, b_send)
    done(bnd, BND, 16, b_sib_send)
    done(pos, 16, 15, p_send)
    done(pos, 16, 16, p_sib_send)
    done(column, COLUMN, 15, h_send)
    done(column, COLUMN, 16, h_sib_send)
    part = tile_z.at[pl.ds(1, N_GRP - 1)]
    pltpu.make_async_copy(part, part, z_send).wait()
    bnd_out.wait()
    column_out.wait()
    remap_out.wait()
    pltpu.make_async_copy(out_buf, out_hbm, out_sem.at[3]).wait()


def finish_kernel(flag_hbm, fast_hbm, node_hbm, ws_hbm, wn_hbm, bnd_hbm, column_hbm, remap_hbm, hub_hbm, src_hbm, dst_hbm,
                  out_hbm,
                  flag, node, ws, wn, bnd, column, remap, hub_ids, edge_src, edge_dst, one_dst, one_src, col_of, summed, degree,
                  out_buf, sem):
    flag_in = pltpu.make_async_copy(flag_hbm, flag, sem.at[0])
    flag_in.start()
    parts = [pl.ds(i * 192, 192) for i in range(4)]
    ins = [pltpu.make_async_copy(fast_hbm.at[p, :], out_buf.at[p, :], sem.at[1 + i]) for i, p in enumerate(parts)]
    outs = [pltpu.make_async_copy(out_buf.at[p, :], out_hbm.at[p, :], sem.at[5 + i]) for i, p in enumerate(parts)]
    for one in ins:
        one.start()
    flag_in.wait()
    for one, two in zip(ins, outs):
        one.wait()
        two.start()
    for two in outs:
        two.wait()

    @pl.when(flag[0, 0] != 0)
    def _():
        grp = lax.axis_index("grp")
        me = lax.axis_index("dev")
        pairs = [(node_hbm, node), (ws_hbm, ws), (wn_hbm, wn), (bnd_hbm, bnd), (column_hbm, column), (remap_hbm, remap),
                 (hub_hbm, hub_ids), (src_hbm, edge_src), (dst_hbm, edge_dst)]
        copies = [pltpu.make_async_copy(a, b, sem.at[i]) for i, (a, b) in enumerate(pairs)]
        for one in copies:
            one.start()
        for one in copies:
            one.wait()
        owner, rank = hub_owner_rank(hub_ids[...])
        at_row = place(owner % N_DEV, me) * COLUMN + ((grp - owner // N_DEV) & 7) * 2 + rank
        choose = jnp.where(lax.broadcasted_iota(I32, (N_DEV * COLUMN, HUBS), 0) == at_row, 1.0, 0.0).astype(BF16)
        hubs = dot(choose, column[...], TN).astype(BF16)
        col_of[...] = edge_column(edge_src[...], me)
        degree[...] = jnp.zeros_like(degree)
        summed[...] = jnp.zeros_like(summed)

        @pl.loop(0, ROWS)
        def _(r):
            here = pl.ds(pl.multiple_of(r * 128, 128), 128)
            match = lax.broadcasted_iota(I32, (NPD, 128), 0) == edge_dst[pl.ds(r, 1), :]
            hit = jnp.where(match, 1.0, 0.0)
            one_dst[:, here] = hit.astype(BF16)
            degree[...] += jnp.sum(hit, axis=1, keepdims=True)

        def block(first, rows):
            n = rows.shape[0]

            @pl.loop(0, ROWS)
            def _(r):
                here = pl.ds(pl.multiple_of(r * 128, 128), 128)
                match = lax.broadcasted_iota(I32, (256, 128), 0) + first == col_of[pl.ds(r, 1), :]
                one_src[:, here] = jnp.where(match, 1.0, 0.0).astype(BF16)

            count = jnp.zeros((NPD, 256), F32)
            for i in range(STEPS):
                here = slice(i * STEP, (i + 1) * STEP)
                count = count + dot(one_dst[:, here], one_src[:, here], NT)
            upper = jnp.floor(count * (1.0 / 256.0)) * 256.0
            lower = count - upper
            summed[...] += dot(upper[:, 0:n].astype(BF16), rows) + dot(lower[:, 0:n].astype(BF16), rows)

        @pl.loop(0, 8)
        def _(g):
            lines = pl.ds(pl.multiple_of(g * 128, 128), 128)
            block(g * 256, dot(remap[lines, :], bnd[lines, :], TN).astype(BF16))

        @pl.loop(0, 3)
        def _(g):
            block(HALO + g * 256, node[pl.ds(pl.multiple_of(g * 256, 256), 256), :])

        block(HALO + NPD, hubs)
        mean = (summed[...] / degree[...]).astype(BF16)
        mixed = dot(node[...], ws[...]) + dot(mean, wn[...])
        out_buf[...] = jnp.maximum(mixed, 0.0).astype(BF16)
        last = pltpu.make_async_copy(out_buf, out_hbm, sem.at[0])
        last.start()
        last.wait()


def body(node_rows, w_self, w_neigh, hub_ids, bnd_idx, send_pos, edge_src, edge_dst):
    any_, vmem = pl.BlockSpec(memory_space=pl.ANY), pl.BlockSpec(memory_space=pltpu.VMEM)
    dma = pltpu.SemaphoreType.DMA
    src, dst = edge_src.reshape(ROWS, 128), edge_dst.reshape(ROWS, 128)
    scratch = [
        pltpu.VMEM((NPD, D), BF16),
        pltpu.VMEM((D, D), BF16),
        pltpu.VMEM((D, D), BF16),
        pltpu.VMEM((N_DEV * BND, D), BF16),
        pltpu.VMEM((N_DEV * 16, 128), BF16),
        pltpu.VMEM((N_DEV * COLUMN, D), BF16),
        pltpu.VMEM((N_GRP, 16, 128), BF16),
        pltpu.VMEM((N_DEV * BND, 256), BF16),
        pltpu.VMEM((ROWS, 128), I32),
        pltpu.VMEM((ROWS, 128), F32),
        pltpu.VMEM((NPD, STEP), BF16),
        pltpu.VMEM((LINES, STEP), BF16),
        pltpu.VMEM((LINES, NPD), F32),
        pltpu.VMEM((NPD, 128), F32),
        pltpu.VMEM((HALO_DIGITS * HALO_LINES, NPD), BF16),
        pltpu.VMEM((NPD, NPD), BF16),
        pltpu.VMEM((HUBS, NPD), BF16),
        pltpu.VMEM((N_DEV * COLUMN, NPD), BF16),
        pltpu.VMEM((N_DEV * BND, NPD), BF16),
        pltpu.VMEM((NPD, D), F32),
        pltpu.VMEM((NPD, D), F32),
        pltpu.VMEM((NPD, D), BF16),
        dma((3,)), dma((4,)), dma, dma, dma, dma, dma, dma, dma, dma((12,)),
    ]
    outs = [
        jax.ShapeDtypeStruct((NPD, D), BF16),
        jax.ShapeDtypeStruct((N_DEV * BND, D), BF16),
        jax.ShapeDtypeStruct((N_DEV * COLUMN, D), BF16),
        jax.ShapeDtypeStruct((N_DEV * BND, 256), BF16),
        jax.ShapeDtypeStruct((8, 128), I32),
    ]
    hub_row = hub_ids.reshape(1, HUBS)
    fast, bnd, column, remap, flag = pl.pallas_call(
        main_kernel,
        out_shape=outs,
        in_specs=[any_, any_, any_, vmem, vmem, vmem, vmem, vmem],
        out_specs=[any_, any_, any_, any_, vmem],
        scratch_shapes=scratch,
        compiler_params=pltpu.CompilerParams(
            collective_id=0, has_side_effects=True, vmem_limit_bytes=56 * 2**20
        ),
        name="sage_main",
    )(node_rows, w_self, w_neigh, hub_row, bnd_idx, send_pos, src, dst)
    scratch = [
        pltpu.SMEM((8, 128), I32),
        pltpu.VMEM((NPD, D), BF16),
        pltpu.VMEM((D, D), BF16),
        pltpu.VMEM((D, D), BF16),
        pltpu.VMEM((N_DEV * BND, D), BF16),
        pltpu.VMEM((N_DEV * COLUMN, D), BF16),
        pltpu.VMEM((N_DEV * BND, 256), BF16),
        pltpu.VMEM((1, HUBS), I32),
        pltpu.VMEM((ROWS, 128), I32),
        pltpu.VMEM((ROWS, 128), I32),
        pltpu.VMEM((NPD, E_DEV), BF16),
        pltpu.VMEM((256, E_DEV), BF16),
        pltpu.VMEM((ROWS, 128), I32),
        pltpu.VMEM((NPD, D), F32),
        pltpu.VMEM((NPD, 1), F32),
        pltpu.VMEM((NPD, D), BF16),
        dma((9,)),
    ]
    return pl.pallas_call(
        finish_kernel,
        out_shape=jax.ShapeDtypeStruct((NPD, D), BF16),
        in_specs=[any_] * 11,
        out_specs=any_,
        scratch_shapes=scratch,
        compiler_params=pltpu.CompilerParams(vmem_limit_bytes=56 * 2**20),
        name="sage_finish",
    )(flag, fast, node_rows, w_self, w_neigh, bnd, column, remap, hub_row, src, dst)


def solution(mesh):
    in_specs = (
        P(("grp", "dev"), None),
        P(),
        P(),
        P(),
        P(("grp", "dev"), None),
        P(("grp", "dev"), None, None),
        P(("grp", "dev")),
        P(("grp", "dev")),
    )
    out_specs = P(("grp", "dev"), None)
    return jax.shard_map(body, mesh=mesh, in_specs=in_specs, out_specs=out_specs, check_vma=False)
```
